512 devices in a mesh: lat: 32 (over y_hi, z), lon: 16 (over y_lo, x, core).
Axes of the slice: x: 4, y: 4 (y_hi: 2, y_lo: 2; y = y_hi * 2 + y_lo), z: 16, core: 2. Of those that a mesh axis runs over, the one named last changes fastest.
Arguments:
- field: bfloat16 [160, 2048, 256], P('lat', 'lon'), may hold values from -6 to 6
- cotangent: bfloat16 [160, 2048, 256], P('lat', 'lon'), may hold values from -6 to 6
- kernel_values: float32 [4, 160, 9, 128], P(None, 'lat'), may hold values from -0.3 to 0.3
- bounds: int32 [2, 160, 9], P(None, 'lat'), may hold values from -63 to 63, as said below
- weight: bfloat16 [1024, 256], replicated, may hold values from -0.1875 to 0.1875
Outputs:
- grad_field: float32 [160, 2048, 256], P('lat', 'lon')
- grad_weight: float32 [1024, 256], replicated
The draws below stay inside these ranges and needn't reach their ends.
Inputs may be any that keep to these rules, and one draw needn't show every extreme that they name: bounds[0] <= 0 <= bounds[1]; some entry has magnitude 64 - 1 in every draw.
All inputs are finite; a program needn't handle non-finite values.
Results may differ from the reference program's by a relative error of at most 0.0041.
Values may be sent and summed in bfloat16 or wider, within the bound.
No kernel may reach another device: no remote copies, remote signals or barrier semaphores. Data moves between devices by JAX's collectives and lax.ppermute only.
A program may use at most 64 MiB of HBM per device.

```python
import math
import jax
import jax.numpy as jnp
from jax import lax

C = 256
K = 4
RAD = 4
NR = 9
HALF = 64
COLS_DEV = 128
LAT = 160
LON = 2048
N_LON = 16


def draw_bounds(key, part):
    key = jax.random.fold_in(key, 11)
    lat_rows = jnp.arange(LAT, dtype=jnp.int32)[:, None]
    row_offset = jnp.abs(jnp.arange(NR, dtype=jnp.int32) - RAD)[None, :]
    chord = 4 - 3 * row_offset * row_offset // (RAD * RAD)
    base_reach = jnp.minimum(4 * HALF, 8 + 24 * HALF // (lat_rows + 1))
    widened = base_reach * chord // 4
    jitter = jax.random.randint(key, (2, LAT, NR), 0, 4, dtype=jnp.int32)
    reach = jnp.minimum(HALF - 1, widened[None] + jitter)
    return jnp.stack([-reach[0], reach[1]]).astype(jnp.int32)


def levels(own_key, shape, shards, low, largest):
    factor_of, own = 1.0, jax.random.fold_in(own_key, 6)
    for axis_at, parts in shards:
        heights = jnp.exp(jax.random.uniform(jax.random.fold_in(own, axis_at), (parts,), jnp.float32, low / len(shards), largest / len(shards)))
        factor_of = factor_of * jnp.repeat(heights, shape[axis_at] // parts).reshape([-1 if axis == axis_at else 1 for axis in range(len(shape))])
    return factor_of


def scatter_about(rng, extent, deviation, most, pieces=(), kind=jnp.bfloat16):
    drawn = deviation * jax.random.normal(rng, extent, jnp.float32)
    if pieces:
        drawn = drawn * levels(rng, extent, pieces, -0.22, 0.18)
    return jnp.clip(drawn, -most, most).astype(kind)


def setup_inputs(seed: int = 0) -> dict:
    keys = jax.random.split(jax.random.key(seed), 6)
    return {
        "field": scatter_about(keys[0], (LAT, LON, C), 1.0, 6.0, ((0, 32), (1, 16))),
        "cotangent": scatter_about(keys[1], (LAT, LON, C), 1.0, 6.0, ((0, 32), (1, 16))),
        "kernel_values": scatter_about(keys[2], (K, LAT, NR, 2 * HALF), 0.05, 0.3, ((1, 32),), jnp.float32),
        "bounds": draw_bounds(jax.random.fold_in(keys[5], 71), 0),
        "weight": scatter_about(keys[4], (K * C, C), (K * C) ** -0.5, 0.1875),
    }


def banded(band_line, col_count, ext_width):
    leading = band_line.shape[:-1]
    padded = jnp.concatenate([band_line, jnp.zeros(leading + (ext_width + 1 - band_line.shape[-1],), band_line.dtype)], axis=-1)
    repeated = jnp.tile(padded, (1,) * len(leading) + (col_count,))
    return repeated[..., :col_count * ext_width].reshape(leading + (col_count, ext_width))

def reference(field, cotangent, kernel_values, bounds, weight):
    offsets = jnp.arange(2 * HALF, dtype=jnp.int32) - HALF
    inside = (offsets >= bounds[0][:, :, None]) & (offsets <= bounds[1][:, :, None])
    kernel = jnp.where(inside[None], kernel_values, jnp.zeros_like(kernel_values)).astype(jnp.bfloat16)
    kernel_ext = jnp.pad(kernel, ((0, 0), (RAD, RAD), (0, 0), (0, 0)))
    stacked = jnp.concatenate([field, cotangent], axis=2)
    stacked = jnp.concatenate([stacked[:, LON - HALF:], stacked, stacked[:, :HALF]], axis=1)
    extended = jnp.pad(stacked, ((RAD, RAD), (0, 0), (0, 0)))
    ext_width = COLS_DEV + 2 * HALF
    col_index = (jnp.arange(N_LON, dtype=jnp.int32)[:, None] * COLS_DEV + jnp.arange(ext_width, dtype=jnp.int32)[None, :]).astype(jnp.int32)
    mixing = weight.astype(jnp.float32).reshape(K, C, C)

    def one_row(running, row_step):
        window = lax.dynamic_slice_in_dim(extended, row_step, NR, 0)
        blocks = jnp.take(window, col_index, axis=1).astype(jnp.float32)
        kernel_slab = lax.dynamic_slice_in_dim(kernel_ext, row_step, NR, 1)
        forward_band = banded(kernel_slab[:, RAD], COLS_DEV, ext_width).astype(jnp.float32)
        basis_row = jnp.einsum('krij,rbjc->bikc', forward_band, blocks[..., :C]).astype(jnp.bfloat16)
        basis_row = basis_row.reshape(N_LON, COLS_DEV, K * C)
        cot_own = blocks[RAD, :, HALF:HALF + COLS_DEV, C:]
        running = running + jnp.einsum('bip,bio->po', basis_row.astype(jnp.float32), cot_own)
        diag_rows = jnp.moveaxis(jnp.diagonal(kernel_slab[:, :, ::-1, :], axis1=1, axis2=2), -1, 1)
        band_line = jnp.concatenate([jnp.zeros(diag_rows.shape[:2] + (1,), diag_rows.dtype), diag_rows[..., ::-1]], axis=-1)
        back_band = banded(band_line, COLS_DEV, ext_width).astype(jnp.float32)
        spread = jnp.einsum('ksji,sbic->bjkc', back_band, blocks[..., C:]).astype(jnp.bfloat16)
        grad_row = jnp.einsum('bjko,kio->bji', spread.astype(jnp.float32), mixing).reshape(LON, C)
        return (running, grad_row)
    zero_sum = jnp.zeros((K * C, C), jnp.float32)
    running, grad_rows = lax.scan(one_row, zero_sum, jnp.arange(LAT, dtype=jnp.int32))
    return (grad_rows, running * (1.0 / math.sqrt(LAT * LON)))
```

```python
import functools
import math

import jax
import jax.numpy as jnp
from jax import lax
from jax.experimental import pallas as pl
from jax.experimental.pallas import tpu as pltpu
from jax.sharding import Mesh, PartitionSpec as P

LAT_AXES = ("yh", "z")
LON_AXES = ("yl", "x", "core")
PLANE = ("yh", "yl", "x", "core")

ROWS, COLS, CH, NK, NR, RAD, HALF = 5, 128, 256, 4, 9, 4, 64
EXT = ROWS + 2 * RAD
LINES = NK * NR


def shifted(x, axes, step, closed):
    count = 1
    for a in axes:
        count *= lax.axis_size(a)
    if closed:
        pairs = [(i, (i + step) % count) for i in range(count)]
    else:
        pairs = [(i, i + step) for i in range(count) if 0 <= i + step < count]
    return lax.ppermute(x, axes, pairs)


def reverse_lines(up_ref, own_ref, down_ref, lines_ref):
    i = lax.broadcasted_iota(jnp.int32, (COLS, COLS), 0)
    j = lax.broadcasted_iota(jnp.int32, (COLS, COLS), 1)
    flip = ((i + j == 0) | (i + j == COLS)).astype(jnp.bfloat16)
    at = 0
    for ref in (up_ref, own_ref, down_ref):
        n = ref.shape[0]
        lines_ref[at : at + n, :] = jnp.dot(
            ref[...].astype(jnp.bfloat16), flip, preferred_element_type=jnp.float32
        )
        at += n


def own_mask():
    n = lax.broadcasted_iota(jnp.int32, (COLS, COLS), 0)
    i = lax.broadcasted_iota(jnp.int32, (COLS, COLS), 1)
    return ((i >= HALF) & (i > n)) | ((i < HALF) & (i <= n))


def fill_band(band_ref, lines_ref, mask, l):
    for k in range(NK):
        for s in range(NR):
            at = LINES * (l + s) + NR * k + NR - 1 - s
            row = jnp.broadcast_to(lines_ref[pl.ds(at, 1), :], (16, COLS))
            base = pltpu.roll(row, 0, 1, stride=1, stride_axis=0).astype(jnp.bfloat16)
            for g in range(COLS // 16):
                tile = base if g == 0 else pltpu.roll(base, 16 * g, 1)
                band_ref[
                    k * COLS + 16 * g : k * COLS + 16 * (g + 1), s * COLS : (s + 1) * COLS
                ] = tile * mask[16 * g : 16 * (g + 1), :]


def inner_kernel(kup, kown, kdown, cup, cown, cdown, part_ref, lines, cells, bands):
    reverse_lines(kup, kown, kdown, lines)
    at = 0
    for ref in (cup, cown, cdown):
        for row in range(ref.shape[0]):
            cells[at : at + HALF, :] = ref[row, HALF:, :]
            cells[at + HALF : at + COLS, :] = ref[row, :HALF, :]
            at += COLS
    mask = own_mask().astype(jnp.bfloat16)
    for l in range(ROWS):
        band = bands.at[l % 2]
        fill_band(band, lines, mask, l)
        part_ref[l] = jnp.dot(
            band[...],
            cells[l * COLS : (l + NR) * COLS, :],
            preferred_element_type=jnp.float32,
        )


def outer_kernel(
    scale, kup, kown, kdown, left, right, part_ref, field_t, mixing, grad_ref, gw_ref,
    lines, cells, bands, spreads,
):
    reverse_lines(kup, kown, kdown, lines)
    for row in range(EXT):
        cells[row * COLS : row * COLS + HALF, :] = left[row]
        cells[row * COLS + HALF : (row + 1) * COLS, :] = right[row]
    mask = 1.0 - own_mask().astype(jnp.float32)
    mask = mask.astype(jnp.bfloat16)
    for l in range(ROWS):
        band = bands.at[l % 2]
        fill_band(band, lines, mask, l)
        spread = part_ref[l] + jnp.dot(
            band[...],
            cells[l * COLS : (l + NR) * COLS, :],
            preferred_element_type=jnp.float32,
        )
        spread = spread.astype(jnp.bfloat16)
        grad = jnp.zeros((COLS, CH), jnp.float32)
        for k in range(NK):
            one = spread[k * COLS : (k + 1) * COLS, :]
            spreads[k, l * COLS : (l + 1) * COLS, :] = one
            grad += jnp.dot(
                one, mixing[k * CH : (k + 1) * CH, :], preferred_element_type=jnp.float32
            )
        grad_ref[l] = grad
    for k in range(NK):
        total = jnp.dot(field_t[...], spreads[k], preferred_element_type=jnp.float32)
        gw_ref[k * CH : (k + 1) * CH, :] = (total * scale).astype(jnp.bfloat16)


def exchange(x, axes):
    return lax.all_to_all(x, axes, 0, 0, tiled=True)


def per_device(field, cotangent, kernel_values, bounds, weight):
    sizes = {a: lax.axis_size(a) for a in LAT_AXES + LON_AXES}
    lat_count = sizes["yh"] * sizes["z"]
    lon_count = sizes["yl"] * sizes["x"] * sizes["core"]
    offsets = jnp.arange(2 * HALF, dtype=jnp.int32) - HALF
    inside = (offsets >= bounds[0][:, :, None]) & (offsets <= bounds[1][:, :, None])
    kernel = jnp.where(inside[None], kernel_values, jnp.zeros_like(kernel_values))
    kernel = kernel.astype(jnp.bfloat16)
    lines = jnp.swapaxes(kernel, 0, 1).reshape(ROWS, LINES, COLS)

    kup = shifted(lines[ROWS - RAD :], LAT_AXES, 1, False)
    kdown = shifted(lines[:RAD], LAT_AXES, -1, False)
    cup = shifted(cotangent[ROWS - RAD :], LAT_AXES, 1, False)
    cdown = shifted(cotangent[:RAD], LAT_AXES, -1, False)
    kargs = (
        kup.reshape(RAD * LINES, COLS),
        lines.reshape(ROWS * LINES, COLS),
        kdown.reshape(RAD * LINES, COLS),
    )
    tall = jnp.concatenate([cup, cotangent, cdown], axis=0)
    left = shifted(tall[:, HALF:], LON_AXES, 1, True)
    right = shifted(tall[:, :HALF], LON_AXES, -1, True)

    params = pltpu.CompilerParams(vmem_limit_bytes=48 * 1024 * 1024)
    scratch = [
        pltpu.VMEM((EXT * LINES, COLS), jnp.float32),
        pltpu.VMEM((EXT * COLS, CH), jnp.bfloat16),
        pltpu.VMEM((2, NK * COLS, NR * COLS), jnp.bfloat16),
    ]
    band_flops = 2 * ROWS * NK * COLS * NR * COLS * CH
    part = pl.pallas_call(
        inner_kernel,
        out_shape=jax.ShapeDtypeStruct((ROWS, NK * COLS, CH), jnp.float32),
        scratch_shapes=scratch,
        compiler_params=params,
        cost_estimate=pl.CostEstimate(
            flops=band_flops, bytes_accessed=4 * 1024 * 1024, transcendentals=0
        ),
        name="inner_band",
    )(*kargs, cup, cotangent, cdown)

    field_t = field.reshape(ROWS * COLS, CH).T
    mixing = jnp.swapaxes(weight.reshape(NK, CH, CH), 1, 2).reshape(NK * CH, CH)
    scale = 1.0 / math.sqrt(ROWS * lat_count * COLS * lon_count)
    grad_field, gw = pl.pallas_call(
        functools.partial(outer_kernel, scale),
        out_shape=(
            jax.ShapeDtypeStruct((ROWS, COLS, CH), jnp.float32),
            jax.ShapeDtypeStruct((NK * CH, CH), jnp.bfloat16),
        ),
        scratch_shapes=scratch + [pltpu.VMEM((NK, ROWS * COLS, CH), jnp.bfloat16)],
        compiler_params=params,
        cost_estimate=pl.CostEstimate(
            flops=band_flops * 2, bytes_accessed=6 * 1024 * 1024, transcendentals=0
        ),
        name="outer_band",
    )(*kargs, left, right, part, field_t, mixing)

    plane, depth = sizes["yh"] * lon_count, sizes["z"]
    piece = gw.shape[0] // plane
    got = exchange(gw.reshape(plane, piece, CH), PLANE)
    mine = jnp.sum(got.astype(jnp.float32), axis=0).astype(jnp.bfloat16)
    got = exchange(jnp.broadcast_to(mine[None], (depth, piece, CH)), "z")
    mine = jnp.sum(got.astype(jnp.float32), axis=0).astype(jnp.bfloat16)
    got = exchange(jnp.broadcast_to(mine[None], (plane, piece, CH)), PLANE)
    return (grad_field, got.reshape(NK * CH, CH).astype(jnp.float32))


def solution(mesh):
    fine = Mesh(mesh.devices.reshape(2, 16, 2, 4, 2), LAT_AXES + LON_AXES)
    return jax.shard_map(
        per_device,
        mesh=fine,
        in_specs=(
            P(LAT_AXES, LON_AXES, None),
            P(LAT_AXES, LON_AXES, None),
            P(None, LAT_AXES, None, None),
            P(None, LAT_AXES, None),
            P(),
        ),
        out_specs=(P(LAT_AXES, LON_AXES, None), P()),
        check_vma=False,
    )
```

```python
import functools
import math

import jax
import jax.numpy as jnp
from jax import lax
from jax.experimental import pallas as pl
from jax.experimental.pallas import tpu as pltpu
from jax.sharding import Mesh, PartitionSpec as P

LAT_AXES = ("yh", "z")
LON_AXES = ("yl", "x", "core")
PLANE = ("yh", "yl", "x", "core")

ROWS, COLS, CH, NK, NR, RAD, HALF = 5, 128, 256, 4, 9, 4, 64
EXT = ROWS + 2 * RAD
LINES = NK * NR
LINES_ROWS = RAD * LINES // 2
PACKED = RAD * COLS + 80


def shifted(x, axes, step, closed):
    count = 1
    for a in axes:
        count *= lax.axis_size(a)
    if closed:
        pairs = [(i, (i + step) % count) for i in range(count)]
    else:
        pairs = [(i, i + step) for i in range(count) if 0 <= i + step < count]
    return lax.ppermute(x, axes, pairs)


def prep_kernel(bounds_ref, values_ref, cells_ref, up_ref, down_ref, own_ref, lines):
    offset = lax.broadcasted_iota(jnp.int32, (NK, COLS), 1) - HALF
    for l in range(ROWS):
        for r in range(NR):
            inside = (offset >= bounds_ref[0, l, r]) & (offset <= bounds_ref[1, l, r])
            at = LINES * l + NK * r
            lines[at : at + NK, :] = jnp.where(inside, values_ref[l, r], 0.0)
    lines[ROWS * LINES :, :] = jnp.zeros((192 - ROWS * LINES, COLS), jnp.float32)
    i = lax.broadcasted_iota(jnp.int32, (COLS, COLS), 0)
    j = lax.broadcasted_iota(jnp.int32, (COLS, COLS), 1)
    flip = ((i + j == 0) | (i + j == COLS)).astype(jnp.bfloat16)
    own_ref[...] = jnp.dot(
        lines[...].astype(jnp.bfloat16), flip, preferred_element_type=jnp.float32
    )
    for ref, row in ((up_ref, ROWS - RAD), (down_ref, 0)):
        for n in range(RAD):
            ref[n * COLS : (n + 1) * COLS, :] = cells_ref[row + n]
        for half in range(2):
            at = LINES * row + half * LINES_ROWS
            ref[RAD * COLS : RAD * COLS + LINES_ROWS, half * COLS : (half + 1) * COLS] = own_ref[
                at : at + LINES_ROWS, :
            ].astype(jnp.bfloat16)
        ref[RAD * COLS + LINES_ROWS :, :] = jnp.zeros(
            (PACKED - RAD * COLS - LINES_ROWS, CH), jnp.bfloat16
        )


def middle_kernel(up_ref, own_ref, down_ref, east_ref, west_ref):
    for row in range(EXT):
        if row < RAD:
            cells = up_ref[row * COLS : (row + 1) * COLS, :]
        elif row < RAD + ROWS:
            cells = own_ref[row - RAD]
        else:
            at = (row - RAD - ROWS) * COLS
            cells = down_ref[at : at + COLS, :]
        east_ref[row] = cells[HALF:]
        west_ref[row] = cells[:HALF]


def gather_lines(up_ref, own_ref, down_ref, lines_ref):
    for ref, at in ((up_ref, 0), (down_ref, (RAD + ROWS) * LINES)):
        for half in range(2):
            lines_ref[at + half * LINES_ROWS : at + (half + 1) * LINES_ROWS, :] = ref[
                RAD * COLS : RAD * COLS + LINES_ROWS, half * COLS : (half + 1) * COLS
            ].astype(jnp.float32)
    lines_ref[RAD * LINES : (RAD + ROWS) * LINES, :] = own_ref[: ROWS * LINES, :]


def own_mask():
    n = lax.broadcasted_iota(jnp.int32, (COLS, COLS), 0)
    i = lax.broadcasted_iota(jnp.int32, (COLS, COLS), 1)
    return ((i >= HALF) & (i > n)) | ((i < HALF) & (i <= n))


def fill_band(band_ref, lines_ref, mask, l):
    for k in range(NK):
        for s in range(NR):
            at = LINES * (l + s) + NK * (NR - 1 - s) + k
            row = jnp.broadcast_to(lines_ref[pl.ds(at, 1), :], (16, COLS))
            base = pltpu.roll(row, 0, 1, stride=1, stride_axis=0).astype(jnp.bfloat16)
            for g in range(COLS // 16):
                tile = base if g == 0 else pltpu.roll(base, 16 * g, 1)
                band_ref[
                    k * COLS + 16 * g : k * COLS + 16 * (g + 1), s * COLS : (s + 1) * COLS
                ] = tile * mask[16 * g : 16 * (g + 1), :]


def inner_kernel(up_ref, lines_own, down_ref, own_ref, part_ref, lines, cells, bands):
    gather_lines(up_ref, lines_own, down_ref, lines)
    for row in range(EXT):
        if row < RAD:
            one = up_ref[row * COLS : (row + 1) * COLS, :]
        elif row < RAD + ROWS:
            one = own_ref[row - RAD]
        else:
            at = (row - RAD - ROWS) * COLS
            one = down_ref[at : at + COLS, :]
        cells[row * COLS : row * COLS + HALF, :] = one[HALF:]
        cells[row * COLS + HALF : (row + 1) * COLS, :] = one[:HALF]
    mask = own_mask().astype(jnp.bfloat16)
    for l in range(ROWS):
        band = bands.at[l % 2]
        fill_band(band, lines, mask, l)
        part_ref[l] = jnp.dot(
            band[...],
            cells[l * COLS : (l + NR) * COLS, :],
            preferred_element_type=jnp.float32,
        )


def outer_kernel(
    scale, up_ref, lines_own, down_ref, left, right, part_ref, field_t, mixing, grad_ref, gw_ref,
    lines, cells, bands, spreads,
):
    gather_lines(up_ref, lines_own, down_ref, lines)
    for row in range(EXT):
        cells[row * COLS : row * COLS + HALF, :] = left[row]
        cells[row * COLS + HALF : (row + 1) * COLS, :] = right[row]
    mask = 1.0 - own_mask().astype(jnp.float32)
    mask = mask.astype(jnp.bfloat16)
    for l in range(ROWS):
        band = bands.at[l % 2]
        fill_band(band, lines, mask, l)
        spread = part_ref[l] + jnp.dot(
            band[...],
            cells[l * COLS : (l + NR) * COLS, :],
            preferred_element_type=jnp.float32,
        )
        spread = spread.astype(jnp.bfloat16)
        grad = jnp.zeros((COLS, CH), jnp.float32)
        for k in range(NK):
            one = spread[k * COLS : (k + 1) * COLS, :]
            spreads[k, l * COLS : (l + 1) * COLS, :] = one
            grad += jnp.dot(
                one, mixing[k * CH : (k + 1) * CH, :], preferred_element_type=jnp.float32
            )
        grad_ref[l] = grad
    for k in range(NK):
        total = jnp.dot(field_t[...], spreads[k], preferred_element_type=jnp.float32)
        gw_ref[k * CH : (k + 1) * CH, :] = (total * scale).astype(jnp.bfloat16)


def exchange(x, axes):
    return lax.all_to_all(x, axes, 0, 0, tiled=True)


def per_device(field, cotangent, kernel_values, bounds, weight):
    sizes = {a: lax.axis_size(a) for a in LAT_AXES + LON_AXES}
    lat_count = sizes["yh"] * sizes["z"]
    lon_count = sizes["yl"] * sizes["x"] * sizes["core"]
    params = pltpu.CompilerParams(vmem_limit_bytes=24 * 1024 * 1024)
    vmem = pl.BlockSpec(memory_space=pltpu.VMEM)
    packed = jax.ShapeDtypeStruct((PACKED, CH), jnp.bfloat16)
    up, down, lines_own = pl.pallas_call(
        prep_kernel,
        out_shape=(packed, packed, jax.ShapeDtypeStruct((192, COLS), jnp.float32)),
        in_specs=[pl.BlockSpec(memory_space=pltpu.SMEM), vmem, vmem],
        scratch_shapes=[pltpu.VMEM((192, COLS), jnp.float32)],
        compiler_params=params,
        name="prep",
    )(bounds, jnp.transpose(kernel_values, (1, 2, 0, 3)), cotangent)
    up = shifted(up, LAT_AXES, 1, False)
    down = shifted(down, LAT_AXES, -1, False)
    side = jax.ShapeDtypeStruct((EXT, HALF, CH), jnp.bfloat16)
    east, west = pl.pallas_call(
        middle_kernel, out_shape=(side, side), compiler_params=params, name="middle"
    )(up, cotangent, down)
    left = shifted(east, LON_AXES, 1, True)
    right = shifted(west, LON_AXES, -1, True)

    scratch = [
        pltpu.VMEM((EXT * LINES, COLS), jnp.float32),
        pltpu.VMEM((EXT * COLS, CH), jnp.bfloat16),
        pltpu.VMEM((2, NK * COLS, NR * COLS), jnp.bfloat16),
    ]
    band_flops = 2 * ROWS * NK * COLS * NR * COLS * CH
    part = pl.pallas_call(
        inner_kernel,
        out_shape=jax.ShapeDtypeStruct((ROWS, NK * COLS, CH), jnp.float32),
        scratch_shapes=scratch,
        compiler_params=params,
        cost_estimate=pl.CostEstimate(
            flops=band_flops, bytes_accessed=4 * 1024 * 1024, transcendentals=0
        ),
        name="inner_band",
    )(up, lines_own, down, cotangent)

    field_t = field.reshape(ROWS * COLS, CH).T
    mixing = jnp.swapaxes(weight.reshape(NK, CH, CH), 1, 2).reshape(NK * CH, CH)
    scale = 1.0 / math.sqrt(ROWS * lat_count * COLS * lon_count)
    grad_field, gw = pl.pallas_call(
        functools.partial(outer_kernel, scale),
        out_shape=(
            jax.ShapeDtypeStruct((ROWS, COLS, CH), jnp.float32),
            jax.ShapeDtypeStruct((NK * CH, CH), jnp.bfloat16),
        ),
        scratch_shapes=scratch + [pltpu.VMEM((NK, ROWS * COLS, CH), jnp.bfloat16)],
        compiler_params=params,
        cost_estimate=pl.CostEstimate(
            flops=band_flops * 2, bytes_accessed=6 * 1024 * 1024, transcendentals=0
        ),
        name="outer_band",
    )(up, lines_own, down, left, right, part, field_t, mixing)

    plane, depth = sizes["yh"] * lon_count, sizes["z"]
    piece = gw.shape[0] // plane
    got = exchange(gw.reshape(plane, piece, CH), PLANE)
    mine = jnp.sum(got.astype(jnp.float32), axis=0).astype(jnp.bfloat16)
    got = exchange(jnp.broadcast_to(mine[None], (depth, piece, CH)), "z")
    mine = jnp.sum(got.astype(jnp.float32), axis=0).astype(jnp.bfloat16)
    got = exchange(jnp.broadcast_to(mine[None], (plane, piece, CH)), PLANE)
    return (grad_field, got.reshape(NK * CH, CH).astype(jnp.float32))


def solution(mesh):
    fine = Mesh(mesh.devices.reshape(2, 16, 2, 4, 2), LAT_AXES + LON_AXES)
    return jax.shard_map(
        per_device,
        mesh=fine,
        in_specs=(
            P(LAT_AXES, LON_AXES, None),
            P(LAT_AXES, LON_AXES, None),
            P(None, LAT_AXES, None, None),
            P(None, LAT_AXES, None),
            P(),
        ),
        out_specs=(P(LAT_AXES, LON_AXES, None), P()),
        check_vma=False,
    )
```

```python
import functools
import math

import jax
import jax.numpy as jnp
from jax import lax
from jax.experimental import pallas as pl
from jax.experimental.pallas import tpu as pltpu
from jax.sharding import Mesh, PartitionSpec as P

LAT_AXES = ("yh", "z")
LON_AXES = ("yl", "x", "core")
PLANE = ("yh", "yl", "x", "core")

ROWS, COLS, CH, NK, NR, RAD, HALF = 5, 128, 256, 4, 9, 4, 64
EXT = ROWS + 2 * RAD
LINES = NK * NR
LINES_ROWS = RAD * LINES // 2
PACKED = RAD * COLS + 80
VMEM_LIMIT = 32 * 1024 * 1024


def shifted(x, axes, step, closed):
    count = 1
    for a in axes:
        count *= lax.axis_size(a)
    if closed:
        pairs = [(i, (i + step) % count) for i in range(count)]
    else:
        pairs = [(i, i + step) for i in range(count) if 0 <= i + step < count]
    return lax.ppermute(x, axes, pairs)


def prep_kernel(
    bounds_hbm, values_hbm, cells_hbm, up_ref, down_ref, own_ref, bounds, values, lines, sems
):
    cell_rows = RAD * COLS
    copies = [
        pltpu.make_async_copy(bounds_hbm, bounds, sems.at[0]),
        pltpu.make_async_copy(values_hbm, values, sems.at[1]),
        pltpu.make_async_copy(
            cells_hbm.at[pl.ds((ROWS - RAD) * COLS, cell_rows)],
            up_ref.at[pl.ds(0, cell_rows)],
            sems.at[2],
        ),
        pltpu.make_async_copy(
            cells_hbm.at[pl.ds(0, cell_rows)], down_ref.at[pl.ds(0, cell_rows)], sems.at[3]
        ),
    ]
    for copy in copies:
        copy.start()
    copies[0].wait()
    copies[1].wait()
    offset = lax.broadcasted_iota(jnp.int32, (NK, COLS), 1) - HALF
    for l in range(ROWS):
        for r in range(NR):
            inside = (offset >= bounds[l, 0, r]) & (offset <= bounds[l, 1, r])
            at = LINES * l + NK * r
            lines[at : at + NK, :] = jnp.where(inside, values[l, r], 0.0)
    lines[ROWS * LINES :, :] = jnp.zeros((192 - ROWS * LINES, COLS), jnp.float32)
    i = lax.broadcasted_iota(jnp.int32, (COLS, COLS), 0)
    j = lax.broadcasted_iota(jnp.int32, (COLS, COLS), 1)
    flip = ((i + j == 0) | (i + j == COLS)).astype(jnp.bfloat16)
    own_ref[...] = jnp.dot(
        lines[...].astype(jnp.bfloat16), flip, preferred_element_type=jnp.float32
    )
    for ref, row in ((up_ref, ROWS - RAD), (down_ref, 0)):
        for half in range(2):
            at = LINES * row + half * LINES_ROWS
            ref[cell_rows : cell_rows + LINES_ROWS, half * COLS : (half + 1) * COLS] = own_ref[
                at : at + LINES_ROWS, :
            ].astype(jnp.bfloat16)
        ref[cell_rows + LINES_ROWS :, :] = jnp.zeros(
            (PACKED - cell_rows - LINES_ROWS, CH), jnp.bfloat16
        )
    copies[2].wait()
    copies[3].wait()


def rows_in_reach(up_ref, up_own, down_own, down_ref):
    for n in range(RAD):
        yield up_ref[n * COLS : (n + 1) * COLS, :]
    yield down_own[:COLS, :]
    for ref in (up_own, down_ref):
        for n in range(RAD):
            yield ref[n * COLS : (n + 1) * COLS, :]


def middle_kernel(up_ref, up_own, down_own, down_ref, east_ref, west_ref):
    for row, cells in enumerate(rows_in_reach(up_ref, up_own, down_own, down_ref)):
        east_ref[row] = cells[HALF:]
        west_ref[row] = cells[:HALF]


def gather_lines(up_ref, own_ref, down_ref, lines_ref):
    for ref, at in ((up_ref, 0), (down_ref, (RAD + ROWS) * LINES)):
        for half in range(2):
            lines_ref[at + half * LINES_ROWS : at + (half + 1) * LINES_ROWS, :] = ref[
                RAD * COLS : RAD * COLS + LINES_ROWS, half * COLS : (half + 1) * COLS
            ].astype(jnp.float32)
    lines_ref[RAD * LINES : (RAD + ROWS) * LINES, :] = own_ref[: ROWS * LINES, :]


def own_mask():
    n = lax.broadcasted_iota(jnp.int32, (COLS, COLS), 0)
    i = lax.broadcasted_iota(jnp.int32, (COLS, COLS), 1)
    return ((i >= HALF) & (i > n)) | ((i < HALF) & (i <= n))


def fill_bands(inner_ref, outer_ref, lines_ref, inner_mask, outer_mask, l):
    for k in range(NK):
        for s in range(NR):
            at = LINES * (l + s) + NK * (NR - 1 - s) + k
            row = jnp.broadcast_to(lines_ref[pl.ds(at, 1), :], (16, COLS))
            base = pltpu.roll(row, 0, 1, stride=1, stride_axis=0).astype(jnp.bfloat16)
            for g in range(COLS // 16):
                tile = base if g == 0 else pltpu.roll(base, 16 * g, 1)
                rows = slice(k * COLS + 16 * g, k * COLS + 16 * (g + 1))
                cols = slice(s * COLS, (s + 1) * COLS)
                inner_ref[rows, cols] = tile * inner_mask[16 * g : 16 * (g + 1), :]
                outer_ref[rows, cols] = tile * outer_mask[16 * g : 16 * (g + 1), :]


def inner_kernel(
    up_ref, up_own, down_own, down_ref, lines_own, part_ref, outer_ref, lines, cells, bands
):
    gather_lines(up_ref, lines_own, down_ref, lines)
    for row, one in enumerate(rows_in_reach(up_ref, up_own, down_own, down_ref)):
        cells[row * COLS : row * COLS + HALF, :] = one[HALF:]
        cells[row * COLS + HALF : (row + 1) * COLS, :] = one[:HALF]
    mask = own_mask().astype(jnp.float32)
    inner_mask, outer_mask = mask.astype(jnp.bfloat16), (1.0 - mask).astype(jnp.bfloat16)
    for l in range(ROWS):
        band = bands.at[l % 2]
        fill_bands(band, outer_ref.at[l], lines, inner_mask, outer_mask, l)
        part_ref[l] = jnp.dot(
            band[...],
            cells[l * COLS : (l + NR) * COLS, :],
            preferred_element_type=jnp.float32,
        )


def outer_kernel(
    scale, bands, left, right, part_ref, field_t, mixing, grad_ref, gw_ref, cells, spreads
):
    for row in range(EXT):
        cells[row * COLS : row * COLS + HALF, :] = left[row]
        cells[row * COLS + HALF : (row + 1) * COLS, :] = right[row]
    for l in range(ROWS):
        spread = part_ref[l] + jnp.dot(
            bands[l],
            cells[l * COLS : (l + NR) * COLS, :],
            preferred_element_type=jnp.float32,
        )
        spread = spread.astype(jnp.bfloat16)
        grad = jnp.zeros((COLS, CH), jnp.float32)
        for k in range(NK):
            one = spread[k * COLS : (k + 1) * COLS, :]
            spreads[k, l * COLS : (l + 1) * COLS, :] = one
            grad += jnp.dot(
                one, mixing[k * CH : (k + 1) * CH, :], preferred_element_type=jnp.float32
            )
        grad_ref[l] = grad
    for k in range(NK):
        total = jnp.dot(field_t[...], spreads[k], preferred_element_type=jnp.float32)
        gw_ref[k * CH : (k + 1) * CH, :] = (total * scale).astype(jnp.bfloat16)


def exchange(x, axes):
    return lax.all_to_all(x, axes, 0, 0, tiled=True)


def per_device(field, cotangent, kernel_values, bounds, weight):
    sizes = {a: lax.axis_size(a) for a in LAT_AXES + LON_AXES}
    lat_count = math.prod(sizes[a] for a in LAT_AXES)
    lon_count = math.prod(sizes[a] for a in LON_AXES)
    params = pltpu.CompilerParams(vmem_limit_bytes=VMEM_LIMIT)
    hbm = pl.BlockSpec(memory_space=pltpu.HBM)
    packed = jax.ShapeDtypeStruct((PACKED, CH), jnp.bfloat16)
    up_own, down_own, lines_own = pl.pallas_call(
        prep_kernel,
        out_shape=(packed, packed, jax.ShapeDtypeStruct((192, COLS), jnp.float32)),
        in_specs=[hbm, hbm, hbm],
        scratch_shapes=[
            pltpu.SMEM((ROWS, 2, NR), jnp.int32),
            pltpu.VMEM((ROWS, NR, NK, COLS), jnp.float32),
            pltpu.VMEM((192, COLS), jnp.float32),
            pltpu.SemaphoreType.DMA((4,)),
        ],
        compiler_params=pltpu.CompilerParams(vmem_limit_bytes=60 * 1024 * 1024),
        name="prep",
    )(
        jnp.transpose(bounds, (1, 0, 2)),
        jnp.transpose(kernel_values, (1, 2, 0, 3)),
        cotangent.reshape(ROWS * COLS, CH),
    )
    field_t = field.reshape(ROWS * COLS, CH).T
    mixing = jnp.swapaxes(weight.reshape(NK, CH, CH), 1, 2).reshape(NK * CH, CH)
    up = shifted(up_own, LAT_AXES, 1, False)
    down = shifted(down_own, LAT_AXES, -1, False)
    up, down, field_t, mixing = lax.optimization_barrier((up, down, field_t, mixing))
    side = jax.ShapeDtypeStruct((EXT, HALF, CH), jnp.bfloat16)
    east, west = pl.pallas_call(
        middle_kernel, out_shape=(side, side), compiler_params=params, name="middle"
    )(up, up_own, down_own, down)
    left = shifted(east, LON_AXES, 1, True)
    right = shifted(west, LON_AXES, -1, True)

    cells = pltpu.VMEM((EXT * COLS, CH), jnp.bfloat16)
    band_flops = 2 * ROWS * NK * COLS * NR * COLS * CH
    part, bands = pl.pallas_call(
        inner_kernel,
        out_shape=(
            jax.ShapeDtypeStruct((ROWS, NK * COLS, CH), jnp.float32),
            jax.ShapeDtypeStruct((ROWS, NK * COLS, NR * COLS), jnp.bfloat16),
        ),
        scratch_shapes=[
            pltpu.VMEM((EXT * LINES, COLS), jnp.float32),
            cells,
            pltpu.VMEM((2, NK * COLS, NR * COLS), jnp.bfloat16),
        ],
        compiler_params=params,
        cost_estimate=pl.CostEstimate(
            flops=band_flops, bytes_accessed=4 * 1024 * 1024, transcendentals=0
        ),
        name="inner_band",
    )(up, up_own, down_own, down, lines_own)

    scale = 1.0 / math.sqrt(ROWS * lat_count * COLS * lon_count)
    grad_field, gw = pl.pallas_call(
        functools.partial(outer_kernel, scale),
        out_shape=(
            jax.ShapeDtypeStruct((ROWS, COLS, CH), jnp.float32),
            jax.ShapeDtypeStruct((NK * CH, CH), jnp.bfloat16),
        ),
        scratch_shapes=[cells, pltpu.VMEM((NK, ROWS * COLS, CH), jnp.bfloat16)],
        compiler_params=params,
        cost_estimate=pl.CostEstimate(
            flops=band_flops * 2, bytes_accessed=6 * 1024 * 1024, transcendentals=0
        ),
        name="outer_band",
    )(bands, left, right, part, field_t, mixing)

    plane, depth = sizes["yh"] * lon_count, lat_count // sizes["yh"]
    piece = gw.shape[0] // plane
    got = exchange(gw.reshape(plane, piece, CH), PLANE)
    mine = jnp.sum(got.astype(jnp.float32), axis=0)
    got = exchange(jnp.broadcast_to(mine[None], (depth, piece, CH)), "z")
    mine = jnp.sum(got, axis=0).astype(jnp.bfloat16)
    got = exchange(jnp.broadcast_to(mine[None], (plane, piece, CH)), PLANE)
    return (grad_field, got.reshape(NK * CH, CH).astype(jnp.float32))


def solution(mesh):
    fine = Mesh(mesh.devices.reshape(2, 16, 2, 4, 2), LAT_AXES + LON_AXES)
    return jax.shard_map(
        per_device,
        mesh=fine,
        in_specs=(
            P(LAT_AXES, LON_AXES, None),
            P(LAT_AXES, LON_AXES, None),
            P(None, LAT_AXES, None, None),
            P(None, LAT_AXES, None),
            P(),
        ),
        out_specs=(P(LAT_AXES, LON_AXES, None), P()),
        check_vma=False,
    )
```

```python
import functools
import math

import jax
import jax.numpy as jnp
from jax import lax
from jax.experimental import pallas as pl
from jax.experimental.pallas import tpu as pltpu
from jax.sharding import Mesh, PartitionSpec as P

LAT_AXES = ("yh", "z")
LON_AXES = ("yl", "x", "core")
PLANE = ("yh", "yl", "x", "core")

ROWS, COLS, CH, NK, NR, RAD, HALF = 5, 128, 256, 4, 9, 4, 64
EXT = ROWS + 2 * RAD
LINES = NK * NR
LINES_ROWS = RAD * LINES // 2
PACKED = RAD * COLS + 80
VMEM_LIMIT = 32 * 1024 * 1024


def shifted(x, axes, step, closed):
    count = 1
    for a in axes:
        count *= lax.axis_size(a)
    if closed:
        pairs = [(i, (i + step) % count) for i in range(count)]
    else:
        pairs = [(i, i + step) for i in range(count) if 0 <= i + step < count]
    return lax.ppermute(x, axes, pairs)


def prep_kernel(
    bounds_hbm, values_hbm, cells_hbm, up_ref, down_ref, own_ref, bounds, values, lines, sems
):
    cell_rows = RAD * COLS
    copies = [
        pltpu.make_async_copy(bounds_hbm, bounds, sems.at[0]),
        pltpu.make_async_copy(values_hbm, values, sems.at[1]),
        pltpu.make_async_copy(
            cells_hbm.at[pl.ds((ROWS - RAD) * COLS, cell_rows)],
            up_ref.at[pl.ds(0, cell_rows)],
            sems.at[2],
        ),
        pltpu.make_async_copy(
            cells_hbm.at[pl.ds(0, cell_rows)], down_ref.at[pl.ds(0, cell_rows)], sems.at[3]
        ),
    ]
    for copy in copies:
        copy.start()
    copies[0].wait()
    copies[1].wait()
    offset = lax.broadcasted_iota(jnp.int32, (NK, COLS), 1) - HALF
    for l in range(ROWS):
        for r in range(NR):
            inside = (offset >= bounds[l, 0, r]) & (offset <= bounds[l, 1, r])
            at = LINES * l + NK * r
            lines[at : at + NK, :] = jnp.where(inside, values[l, r], 0.0)
    lines[ROWS * LINES :, :] = jnp.zeros((192 - ROWS * LINES, COLS), jnp.float32)
    i = lax.broadcasted_iota(jnp.int32, (COLS, COLS), 0)
    j = lax.broadcasted_iota(jnp.int32, (COLS, COLS), 1)
    flip = ((i + j == 0) | (i + j == COLS)).astype(jnp.bfloat16)
    own_ref[...] = jnp.dot(
        lines[...].astype(jnp.bfloat16), flip, preferred_element_type=jnp.float32
    )
    for ref, row in ((up_ref, ROWS - RAD), (down_ref, 0)):
        for half in range(2):
            at = LINES * row + half * LINES_ROWS
            ref[cell_rows : cell_rows + LINES_ROWS, half * COLS : (half + 1) * COLS] = own_ref[
                at : at + LINES_ROWS, :
            ].astype(jnp.bfloat16)
        ref[cell_rows + LINES_ROWS :, :] = jnp.zeros(
            (PACKED - cell_rows - LINES_ROWS, CH), jnp.bfloat16
        )
    copies[2].wait()
    copies[3].wait()


def own_kernel(cells_ref, lines_ref, field_ref, weight_ref, own_ref, lines_own, field_t, mixing):
    own_ref[...] = cells_ref[...]
    lines_own[...] = lines_ref[...]
    field_t[...] = field_ref[...].T
    for k in range(NK):
        mixing[k * CH : (k + 1) * CH, :] = weight_ref[k * CH : (k + 1) * CH, :].T


def rows_in_reach(up_ref, own_ref, down_ref):
    for n in range(RAD):
        yield up_ref[n * COLS : (n + 1) * COLS, :]
    for n in range(ROWS):
        yield own_ref[n]
    for n in range(RAD):
        yield down_ref[n * COLS : (n + 1) * COLS, :]


def middle_kernel(up_ref, own_ref, down_ref, east_ref, west_ref):
    for row, cells in enumerate(rows_in_reach(up_ref, own_ref, down_ref)):
        east_ref[row] = cells[HALF:]
        west_ref[row] = cells[:HALF]


def gather_lines(up_ref, own_ref, down_ref, lines_ref):
    for ref, at in ((up_ref, 0), (down_ref, (RAD + ROWS) * LINES)):
        for half in range(2):
            lines_ref[at + half * LINES_ROWS : at + (half + 1) * LINES_ROWS, :] = ref[
                RAD * COLS : RAD * COLS + LINES_ROWS, half * COLS : (half + 1) * COLS
            ].astype(jnp.float32)
    lines_ref[RAD * LINES : (RAD + ROWS) * LINES, :] = own_ref[: ROWS * LINES, :]


def own_mask():
    n = lax.broadcasted_iota(jnp.int32, (COLS, COLS), 0)
    i = lax.broadcasted_iota(jnp.int32, (COLS, COLS), 1)
    return ((i >= HALF) & (i > n)) | ((i < HALF) & (i <= n))


def fill_bands(inner_ref, outer_ref, lines_ref, inner_mask, outer_mask, l):
    for k in range(NK):
        for s in range(NR):
            at = LINES * (l + s) + NK * (NR - 1 - s) + k
            row = jnp.broadcast_to(lines_ref[pl.ds(at, 1), :], (16, COLS))
            base = pltpu.roll(row, 0, 1, stride=1, stride_axis=0).astype(jnp.bfloat16)
            for g in range(COLS // 16):
                tile = base if g == 0 else pltpu.roll(base, 16 * g, 1)
                rows = slice(k * COLS + 16 * g, k * COLS + 16 * (g + 1))
                cols = slice(s * COLS, (s + 1) * COLS)
                inner_ref[rows, cols] = tile * inner_mask[16 * g : 16 * (g + 1), :]
                outer_ref[rows, cols] = tile * outer_mask[16 * g : 16 * (g + 1), :]


def inner_kernel(
    up_ref, own_ref, down_ref, lines_own, part_ref, outer_ref, lines, cells, bands
):
    gather_lines(up_ref, lines_own, down_ref, lines)
    for row, one in enumerate(rows_in_reach(up_ref, own_ref, down_ref)):
        cells[row * COLS : row * COLS + HALF, :] = one[HALF:]
        cells[row * COLS + HALF : (row + 1) * COLS, :] = one[:HALF]
    mask = own_mask().astype(jnp.float32)
    inner_mask, outer_mask = mask.astype(jnp.bfloat16), (1.0 - mask).astype(jnp.bfloat16)
    for l in range(ROWS):
        band = bands.at[l % 2]
        fill_bands(band, outer_ref.at[l], lines, inner_mask, outer_mask, l)
        part_ref[l] = jnp.dot(
            band[...],
            cells[l * COLS : (l + NR) * COLS, :],
            preferred_element_type=jnp.float32,
        )


def outer_kernel(
    scale, bands, left, right, part_ref, field_t, mixing, grad_ref, gw_ref, cells, spreads
):
    for row in range(EXT):
        cells[row * COLS : row * COLS + HALF, :] = left[row]
        cells[row * COLS + HALF : (row + 1) * COLS, :] = right[row]
    for l in range(ROWS):
        window = cells[l * COLS : (l + NR) * COLS, :]
        for k in range(NK):
            rows = slice(k * COLS, (k + 1) * COLS)
            spread = part_ref[l, rows, :] + jnp.dot(
                bands[l, rows, :], window, preferred_element_type=jnp.float32
            )
            spreads[l * COLS : (l + 1) * COLS, k * CH : (k + 1) * CH] = spread.astype(jnp.bfloat16)
    total = jnp.dot(field_t[...], spreads[...], preferred_element_type=jnp.float32) * scale
    for k in range(NK):
        gw_ref[k * CH : (k + 1) * CH, :] = total[:, k * CH : (k + 1) * CH].astype(jnp.bfloat16)
    grad = jnp.dot(spreads[...], mixing[...], preferred_element_type=jnp.float32)
    for l in range(ROWS):
        grad_ref[l] = grad[l * COLS : (l + 1) * COLS, :]


def exchange(x, axes):
    return lax.all_to_all(x, axes, 0, 0, tiled=True)


def per_device(field, cotangent, kernel_values, bounds, weight):
    sizes = {a: lax.axis_size(a) for a in LAT_AXES + LON_AXES}
    lat_count = math.prod(sizes[a] for a in LAT_AXES)
    lon_count = math.prod(sizes[a] for a in LON_AXES)
    params = pltpu.CompilerParams(vmem_limit_bytes=VMEM_LIMIT)
    hbm = pl.BlockSpec(memory_space=pltpu.HBM)
    packed = jax.ShapeDtypeStruct((PACKED, CH), jnp.bfloat16)
    up_own, down_own, lines_own = pl.pallas_call(
        prep_kernel,
        out_shape=(packed, packed, jax.ShapeDtypeStruct((192, COLS), jnp.float32)),
        in_specs=[hbm, hbm, hbm],
        scratch_shapes=[
            pltpu.SMEM((ROWS, 2, NR), jnp.int32),
            pltpu.VMEM((ROWS, NR, NK, COLS), jnp.float32),
            pltpu.VMEM((192, COLS), jnp.float32),
            pltpu.SemaphoreType.DMA((4,)),
        ],
        compiler_params=pltpu.CompilerParams(vmem_limit_bytes=60 * 1024 * 1024),
        name="prep",
    )(
        jnp.transpose(bounds, (1, 0, 2)),
        jnp.transpose(kernel_values, (1, 2, 0, 3)),
        cotangent.reshape(ROWS * COLS, CH),
    )
    own, lines_own, field_t, mixing = pl.pallas_call(
        own_kernel,
        out_shape=(
            jax.ShapeDtypeStruct(cotangent.shape, jnp.bfloat16),
            jax.ShapeDtypeStruct(lines_own.shape, jnp.float32),
            jax.ShapeDtypeStruct((CH, ROWS * COLS), jnp.bfloat16),
            jax.ShapeDtypeStruct((NK * CH, CH), jnp.bfloat16),
        ),
        compiler_params=params,
        cost_estimate=pl.CostEstimate(flops=0, bytes_accessed=4 * 1024 * 1024, transcendentals=0),
        name="own",
    )(cotangent, lines_own, field.reshape(ROWS * COLS, CH), weight)
    up = shifted(up_own, LAT_AXES, 1, False)
    down = shifted(down_own, LAT_AXES, -1, False)
    up, down, own, lines_own, field_t, mixing = lax.optimization_barrier(
        (up, down, own, lines_own, field_t, mixing)
    )
    side = jax.ShapeDtypeStruct((EXT, HALF, CH), jnp.bfloat16)
    east, west = pl.pallas_call(
        middle_kernel, out_shape=(side, side), compiler_params=params, name="middle"
    )(up, own, down)
    left = shifted(east, LON_AXES, 1, True)
    right = shifted(west, LON_AXES, -1, True)

    cells = pltpu.VMEM((EXT * COLS, CH), jnp.bfloat16)
    band_flops = 2 * ROWS * NK * COLS * NR * COLS * CH
    part, bands = pl.pallas_call(
        inner_kernel,
        out_shape=(
            jax.ShapeDtypeStruct((ROWS, NK * COLS, CH), jnp.float32),
            jax.ShapeDtypeStruct((ROWS, NK * COLS, NR * COLS), jnp.bfloat16),
        ),
        scratch_shapes=[
            pltpu.VMEM((EXT * LINES, COLS), jnp.float32),
            cells,
            pltpu.VMEM((2, NK * COLS, NR * COLS), jnp.bfloat16),
        ],
        compiler_params=params,
        cost_estimate=pl.CostEstimate(
            flops=band_flops, bytes_accessed=4 * 1024 * 1024, transcendentals=0
        ),
        name="inner_band",
    )(up, own, down, lines_own)

    scale = 1.0 / math.sqrt(ROWS * lat_count * COLS * lon_count)
    grad_field, gw = pl.pallas_call(
        functools.partial(outer_kernel, scale),
        out_shape=(
            jax.ShapeDtypeStruct((ROWS, COLS, CH), jnp.float32),
            jax.ShapeDtypeStruct((NK * CH, CH), jnp.bfloat16),
        ),
        scratch_shapes=[cells, pltpu.VMEM((ROWS * COLS, NK * CH), jnp.bfloat16)],
        compiler_params=params,
        cost_estimate=pl.CostEstimate(
            flops=band_flops * 2, bytes_accessed=6 * 1024 * 1024, transcendentals=0
        ),
        name="outer_band",
    )(bands, left, right, part, field_t, mixing)

    plane, depth = sizes["yh"] * lon_count, lat_count // sizes["yh"]
    piece = gw.shape[0] // plane
    got = exchange(gw.reshape(plane, piece, CH), PLANE)
    mine = jnp.sum(got.astype(jnp.float32), axis=0).astype(jnp.bfloat16)
    got = exchange(jnp.broadcast_to(mine[None], (depth, piece, CH)), "z")
    mine = jnp.sum(got.astype(jnp.float32), axis=0).astype(jnp.bfloat16)
    got = exchange(jnp.broadcast_to(mine[None], (plane, piece, CH)), PLANE)
    return (grad_field, got.reshape(NK * CH, CH).astype(jnp.float32))


def solution(mesh):
    fine = Mesh(mesh.devices.reshape(2, 16, 2, 4, 2), LAT_AXES + LON_AXES)
    return jax.shard_map(
        per_device,
        mesh=fine,
        in_specs=(
            P(LAT_AXES, LON_AXES, None),
            P(LAT_AXES, LON_AXES, None),
            P(None, LAT_AXES, None, None),
            P(None, LAT_AXES, None),
            P(),
        ),
        out_specs=(P(LAT_AXES, LON_AXES, None), P()),
        check_vma=False,
    )
```

```python
import functools
import math

import jax
import jax.numpy as jnp
from jax import lax
from jax.experimental import pallas as pl
from jax.experimental.pallas import tpu as pltpu
from jax.sharding import Mesh, PartitionSpec as P

LAT_AXES = ("yh", "z")
LON_AXES = ("yl", "x", "core")
PLANE = ("yh", "yl", "x", "core")

ROWS, COLS, CH, NK, NR, RAD, HALF = 5, 128, 256, 4, 9, 4, 64
EXT = ROWS + 2 * RAD
LINES = NK * NR
LINES_ROWS = RAD * LINES // 2
PACKED = RAD * COLS + 80
VMEM_LIMIT = 32 * 1024 * 1024


def shifted(x, axes, step):
    count = math.prod(lax.axis_size(a) for a in axes)
    pairs = [(i, i + step) for i in range(count) if 0 <= i + step < count]
    return lax.ppermute(x, axes, pairs)


def prep_kernel(
    bounds_hbm, values_hbm, cells_hbm, up_ref, down_ref, own_ref, bounds, values, lines, sems
):
    cell_rows = RAD * COLS
    copies = [
        pltpu.make_async_copy(bounds_hbm, bounds, sems.at[0]),
        pltpu.make_async_copy(values_hbm, values, sems.at[1]),
        pltpu.make_async_copy(
            cells_hbm.at[pl.ds((ROWS - RAD) * COLS, cell_rows)],
            up_ref.at[pl.ds(0, cell_rows)],
            sems.at[2],
        ),
        pltpu.make_async_copy(
            cells_hbm.at[pl.ds(0, cell_rows)], down_ref.at[pl.ds(0, cell_rows)], sems.at[3]
        ),
    ]
    for copy in copies:
        copy.start()
    copies[0].wait()
    copies[1].wait()
    offset = lax.broadcasted_iota(jnp.int32, (NK, COLS), 1) - HALF
    for l in range(ROWS):
        for r in range(NR):
            inside = (offset >= bounds[l, 0, r]) & (offset <= bounds[l, 1, r])
            at = LINES * l + NK * r
            lines[at : at + NK, :] = jnp.where(inside, values[l, r], 0.0)
    lines[ROWS * LINES :, :] = jnp.zeros((192 - ROWS * LINES, COLS), jnp.float32)
    i = lax.broadcasted_iota(jnp.int32, (COLS, COLS), 0)
    j = lax.broadcasted_iota(jnp.int32, (COLS, COLS), 1)
    flip = ((i + j == 0) | (i + j == COLS)).astype(jnp.bfloat16)
    own_ref[...] = jnp.dot(
        lines[...].astype(jnp.bfloat16), flip, preferred_element_type=jnp.float32
    )
    for ref, row in ((up_ref, ROWS - RAD), (down_ref, 0)):
        for half in range(2):
            at = LINES * row + half * LINES_ROWS
            ref[cell_rows : cell_rows + LINES_ROWS, half * COLS : (half + 1) * COLS] = own_ref[
                at : at + LINES_ROWS, :
            ].astype(jnp.bfloat16)
        ref[cell_rows + LINES_ROWS :, :] = jnp.zeros(
            (PACKED - cell_rows - LINES_ROWS, CH), jnp.bfloat16
        )
    copies[2].wait()
    copies[3].wait()


def own_kernel(cells_ref, lines_ref, field_ref, weight_ref, own_ref, lines_own, field_t, mixing):
    own_ref[...] = cells_ref[...]
    lines_own[...] = lines_ref[...]
    field_t[...] = field_ref[...].T
    for k in range(NK):
        mixing[k * CH : (k + 1) * CH, :] = weight_ref[k * CH : (k + 1) * CH, :].T


def rows_in_reach(up_ref, own_ref, down_ref):
    for n in range(RAD):
        yield up_ref[n * COLS : (n + 1) * COLS, :]
    for n in range(ROWS):
        yield own_ref[n]
    for n in range(RAD):
        yield down_ref[n * COLS : (n + 1) * COLS, :]


def middle_kernel(up_ref, own_ref, down_ref, across_ref, beside_ref):
    first = pl.multiple_of(lax.axis_index("core") * HALF, HALF)
    other = pl.multiple_of(HALF - first, HALF)
    for n in range(RAD):
        across_ref[n] = up_ref[pl.ds(n * COLS + first, HALF), :]
        beside_ref[n] = up_ref[pl.ds(n * COLS + other, HALF), :]
        across_ref[RAD + ROWS + n] = down_ref[pl.ds(n * COLS + first, HALF), :]
        beside_ref[RAD + ROWS + n] = down_ref[pl.ds(n * COLS + other, HALF), :]
    for n in range(ROWS):
        across_ref[RAD + n] = own_ref[n, pl.ds(first, HALF), :]
        beside_ref[RAD + n] = own_ref[n, pl.ds(other, HALF), :]


def gather_lines(up_ref, own_ref, down_ref, lines_ref):
    for ref, at in ((up_ref, 0), (down_ref, (RAD + ROWS) * LINES)):
        for half in range(2):
            lines_ref[at + half * LINES_ROWS : at + (half + 1) * LINES_ROWS, :] = ref[
                RAD * COLS : RAD * COLS + LINES_ROWS, half * COLS : (half + 1) * COLS
            ].astype(jnp.float32)
    lines_ref[RAD * LINES : (RAD + ROWS) * LINES, :] = own_ref[: ROWS * LINES, :]


def own_mask():
    n = lax.broadcasted_iota(jnp.int32, (COLS, COLS), 0)
    i = lax.broadcasted_iota(jnp.int32, (COLS, COLS), 1)
    return ((i >= HALF) & (i > n)) | ((i < HALF) & (i <= n))


def fill_bands(inner_ref, outer_ref, lines_ref, inner_mask, outer_mask, l):
    for k in range(NK):
        for s in range(NR):
            at = LINES * (l + s) + NK * (NR - 1 - s) + k
            row = jnp.broadcast_to(lines_ref[pl.ds(at, 1), :], (16, COLS))
            base = pltpu.roll(row, 0, 1, stride=1, stride_axis=0).astype(jnp.bfloat16)
            for g in range(COLS // 16):
                tile = base if g == 0 else pltpu.roll(base, 16 * g, 1)
                rows = slice(k * COLS + 16 * g, k * COLS + 16 * (g + 1))
                cols = slice(s * COLS, (s + 1) * COLS)
                inner_ref[rows, cols] = tile * inner_mask[16 * g : 16 * (g + 1), :]
                outer_ref[rows, cols] = tile * outer_mask[16 * g : 16 * (g + 1), :]


def inner_kernel(
    up_ref, own_ref, down_ref, lines_own, part_ref, outer_ref, lines, cells, bands
):
    gather_lines(up_ref, lines_own, down_ref, lines)
    for row, one in enumerate(rows_in_reach(up_ref, own_ref, down_ref)):
        cells[row * COLS : row * COLS + HALF, :] = one[HALF:]
        cells[row * COLS + HALF : (row + 1) * COLS, :] = one[:HALF]
    mask = own_mask().astype(jnp.float32)
    inner_mask, outer_mask = mask.astype(jnp.bfloat16), (1.0 - mask).astype(jnp.bfloat16)
    for l in range(ROWS):
        band = bands.at[l % 2]
        fill_bands(band, outer_ref.at[l], lines, inner_mask, outer_mask, l)
        part_ref[l] = jnp.dot(
            band[...],
            cells[l * COLS : (l + NR) * COLS, :],
            preferred_element_type=jnp.float32,
        )


def outer_kernel(
    scale, bands, across, beside, part_ref, field_t, mixing, grad_ref, gw_ref, cells, spreads
):
    first = pl.multiple_of(lax.axis_index("core") * HALF, HALF)
    other = pl.multiple_of(HALF - first, HALF)
    for row in range(EXT):
        cells[pl.ds(row * COLS + first, HALF), :] = across[row]
        cells[pl.ds(row * COLS + other, HALF), :] = beside[row]
    for l in range(ROWS):
        window = cells[l * COLS : (l + NR) * COLS, :]
        for k in range(NK):
            rows = slice(k * COLS, (k + 1) * COLS)
            spread = part_ref[l, rows, :] + jnp.dot(
                bands[l, rows, :], window, preferred_element_type=jnp.float32
            )
            spreads[l * COLS : (l + 1) * COLS, k * CH : (k + 1) * CH] = spread.astype(jnp.bfloat16)
    total = jnp.dot(field_t[...], spreads[...], preferred_element_type=jnp.float32) * scale
    for k in range(NK):
        gw_ref[k * CH : (k + 1) * CH, :] = total[:, k * CH : (k + 1) * CH].astype(jnp.bfloat16)
    grad = jnp.dot(spreads[...], mixing[...], preferred_element_type=jnp.float32)
    for l in range(ROWS):
        grad_ref[l] = grad[l * COLS : (l + 1) * COLS, :]


def exchange(x, axes):
    return lax.all_to_all(x, axes, 0, 0, tiled=True)


def per_device(field, cotangent, kernel_values, bounds, weight):
    sizes = {a: lax.axis_size(a) for a in LAT_AXES + LON_AXES}
    lat_count = math.prod(sizes[a] for a in LAT_AXES)
    lon_count = math.prod(sizes[a] for a in LON_AXES)
    params = pltpu.CompilerParams(vmem_limit_bytes=VMEM_LIMIT)
    hbm = pl.BlockSpec(memory_space=pltpu.HBM)
    packed = jax.ShapeDtypeStruct((PACKED, CH), jnp.bfloat16)
    up_own, down_own, lines_own = pl.pallas_call(
        prep_kernel,
        out_shape=(packed, packed, jax.ShapeDtypeStruct((192, COLS), jnp.float32)),
        in_specs=[hbm, hbm, hbm],
        scratch_shapes=[
            pltpu.SMEM((ROWS, 2, NR), jnp.int32),
            pltpu.VMEM((ROWS, NR, NK, COLS), jnp.float32),
            pltpu.VMEM((192, COLS), jnp.float32),
            pltpu.SemaphoreType.DMA((4,)),
        ],
        compiler_params=pltpu.CompilerParams(vmem_limit_bytes=60 * 1024 * 1024),
        name="prep",
    )(
        jnp.transpose(bounds, (1, 0, 2)),
        jnp.transpose(kernel_values, (1, 2, 0, 3)),
        cotangent.reshape(ROWS * COLS, CH),
    )
    own, lines_own, field_t, mixing = pl.pallas_call(
        own_kernel,
        out_shape=(
            jax.ShapeDtypeStruct(cotangent.shape, jnp.bfloat16),
            jax.ShapeDtypeStruct(lines_own.shape, jnp.float32),
            jax.ShapeDtypeStruct((CH, ROWS * COLS), jnp.bfloat16),
            jax.ShapeDtypeStruct((NK * CH, CH), jnp.bfloat16),
        ),
        compiler_params=params,
        cost_estimate=pl.CostEstimate(flops=0, bytes_accessed=4 * 1024 * 1024, transcendentals=0),
        name="own",
    )(cotangent, lines_own, field.reshape(ROWS * COLS, CH), weight)
    up = shifted(up_own, LAT_AXES, 1)
    down = shifted(down_own, LAT_AXES, -1)
    up, down, own, lines_own, field_t, mixing = lax.optimization_barrier(
        (up, down, own, lines_own, field_t, mixing)
    )
    side = jax.ShapeDtypeStruct((EXT, HALF, CH), jnp.bfloat16)
    across, beside = pl.pallas_call(
        middle_kernel, out_shape=(side, side), compiler_params=params, name="middle"
    )(up, own, down)
    across = lax.ppermute(
        across, LON_AXES, [(i, (i - 1 + 2 * (i % 2)) % lon_count) for i in range(lon_count)]
    )
    beside = lax.ppermute(beside, "core", [(0, 1), (1, 0)])

    cells = pltpu.VMEM((EXT * COLS, CH), jnp.bfloat16)
    band_flops = 2 * ROWS * NK * COLS * NR * COLS * CH
    part, bands = pl.pallas_call(
        inner_kernel,
        out_shape=(
            jax.ShapeDtypeStruct((ROWS, NK * COLS, CH), jnp.float32),
            jax.ShapeDtypeStruct((ROWS, NK * COLS, NR * COLS), jnp.bfloat16),
        ),
        scratch_shapes=[
            pltpu.VMEM((EXT * LINES, COLS), jnp.float32),
            cells,
            pltpu.VMEM((2, NK * COLS, NR * COLS), jnp.bfloat16),
        ],
        compiler_params=params,
        cost_estimate=pl.CostEstimate(
            flops=band_flops, bytes_accessed=4 * 1024 * 1024, transcendentals=0
        ),
        name="inner_band",
    )(up, own, down, lines_own)

    scale = 1.0 / math.sqrt(ROWS * lat_count * COLS * lon_count)
    grad_field, gw = pl.pallas_call(
        functools.partial(outer_kernel, scale),
        out_shape=(
            jax.ShapeDtypeStruct((ROWS, COLS, CH), jnp.float32),
            jax.ShapeDtypeStruct((NK * CH, CH), jnp.bfloat16),
        ),
        scratch_shapes=[cells, pltpu.VMEM((ROWS * COLS, NK * CH), jnp.bfloat16)],
        compiler_params=params,
        cost_estimate=pl.CostEstimate(
            flops=band_flops * 2, bytes_accessed=6 * 1024 * 1024, transcendentals=0
        ),
        name="outer_band",
    )(bands, across, beside, part, field_t, mixing)

    plane, depth = sizes["yh"] * lon_count, lat_count // sizes["yh"]
    piece = gw.shape[0] // plane
    got = exchange(gw.reshape(plane, piece, CH), PLANE)
    mine = jnp.sum(got.astype(jnp.float32), axis=0).astype(jnp.bfloat16)
    got = exchange(jnp.broadcast_to(mine[None], (depth, piece, CH)), "z")
    mine = jnp.sum(got.astype(jnp.float32), axis=0).astype(jnp.bfloat16)
    got = exchange(jnp.broadcast_to(mine[None], (plane, piece, CH)), PLANE)
    return (grad_field, got.reshape(NK * CH, CH).astype(jnp.float32))


def solution(mesh):
    fine = Mesh(mesh.devices.reshape(2, 16, 2, 4, 2), LAT_AXES + LON_AXES)
    return jax.shard_map(
        per_device,
        mesh=fine,
        in_specs=(
            P(LAT_AXES, LON_AXES, None),
            P(LAT_AXES, LON_AXES, None),
            P(None, LAT_AXES, None, None),
            P(None, LAT_AXES, None),
            P(),
        ),
        out_specs=(P(LAT_AXES, LON_AXES, None), P()),
        check_vma=False,
    )
```

```python
import functools
import math

import jax
import jax.numpy as jnp
from jax import lax
from jax.experimental import pallas as pl
from jax.experimental.pallas import tpu as pltpu
from jax.sharding import Mesh, PartitionSpec as P

LAT_AXES = ("yh", "zh", "zl")
LON_AXES = ("yl", "x", "core")
PLANE = ("yh", "yl", "x", "core")

ROWS, COLS, CH, NK, NR, RAD, HALF = 5, 128, 256, 4, 9, 4, 64
EXT = ROWS + 2 * RAD
LINES = NK * NR
LINES_ROWS = RAD * LINES // 2
PACKED = RAD * COLS + 80
VMEM_LIMIT = 32 * 1024 * 1024


def shifted(x, axes, step):
    count = math.prod(lax.axis_size(a) for a in axes)
    pairs = [(i, i + step) for i in range(count) if 0 <= i + step < count]
    return lax.ppermute(x, axes, pairs)


def prep_kernel(
    bounds_hbm, values_hbm, cells_hbm, up_ref, down_ref, own_ref, bounds, values, lines, sems
):
    cell_rows = RAD * COLS
    copies = [
        pltpu.make_async_copy(bounds_hbm, bounds, sems.at[0]),
        pltpu.make_async_copy(values_hbm, values, sems.at[1]),
        pltpu.make_async_copy(
            cells_hbm.at[pl.ds((ROWS - RAD) * COLS, cell_rows)],
            up_ref.at[pl.ds(0, cell_rows)],
            sems.at[2],
        ),
        pltpu.make_async_copy(
            cells_hbm.at[pl.ds(0, cell_rows)], down_ref.at[pl.ds(0, cell_rows)], sems.at[3]
        ),
    ]
    for copy in copies:
        copy.start()
    copies[0].wait()
    copies[1].wait()
    offset = lax.broadcasted_iota(jnp.int32, (NK, COLS), 1) - HALF
    for l in range(ROWS):
        for r in range(NR):
            inside = (offset >= bounds[l, 0, r]) & (offset <= bounds[l, 1, r])
            at = LINES * l + NK * r
            lines[at : at + NK, :] = jnp.where(inside, values[l, r], 0.0)
    lines[ROWS * LINES :, :] = jnp.zeros((192 - ROWS * LINES, COLS), jnp.float32)
    i = lax.broadcasted_iota(jnp.int32, (COLS, COLS), 0)
    j = lax.broadcasted_iota(jnp.int32, (COLS, COLS), 1)
    flip = ((i + j == 0) | (i + j == COLS)).astype(jnp.bfloat16)
    own_ref[...] = jnp.dot(
        lines[...].astype(jnp.bfloat16), flip, preferred_element_type=jnp.float32
    )
    for ref, row in ((up_ref, ROWS - RAD), (down_ref, 0)):
        for half in range(2):
            at = LINES * row + half * LINES_ROWS
            ref[cell_rows : cell_rows + LINES_ROWS, half * COLS : (half + 1) * COLS] = own_ref[
                at : at + LINES_ROWS, :
            ].astype(jnp.bfloat16)
        ref[cell_rows + LINES_ROWS :, :] = jnp.zeros(
            (PACKED - cell_rows - LINES_ROWS, CH), jnp.bfloat16
        )
    copies[2].wait()
    copies[3].wait()


def own_kernel(cells_ref, lines_ref, field_ref, weight_ref, own_ref, lines_own, field_t, mixing):
    own_ref[...] = cells_ref[...]
    lines_own[...] = lines_ref[...]
    turned = field_ref[...].T
    field_t[:, : ROWS * COLS] = turned
    field_t[:, ROWS * COLS :] = turned
    for k in range(NK):
        mixing[k * CH : (k + 1) * CH, :] = weight_ref[k * CH : (k + 1) * CH, :].T


def rows_in_reach(up_ref, own_ref, down_ref):
    for n in range(RAD):
        yield up_ref[n * COLS : (n + 1) * COLS, :]
    for n in range(ROWS):
        yield own_ref[n]
    for n in range(RAD):
        yield down_ref[n * COLS : (n + 1) * COLS, :]


def middle_kernel(up_ref, own_ref, down_ref, across_ref, beside_ref):
    first = pl.multiple_of(lax.axis_index("core") * HALF, HALF)
    other = pl.multiple_of(HALF - first, HALF)
    for n in range(RAD):
        across_ref[n] = up_ref[pl.ds(n * COLS + first, HALF), :]
        beside_ref[n] = up_ref[pl.ds(n * COLS + other, HALF), :]
        across_ref[RAD + ROWS + n] = down_ref[pl.ds(n * COLS + first, HALF), :]
        beside_ref[RAD + ROWS + n] = down_ref[pl.ds(n * COLS + other, HALF), :]
    for n in range(ROWS):
        across_ref[RAD + n] = own_ref[n, pl.ds(first, HALF), :]
        beside_ref[RAD + n] = own_ref[n, pl.ds(other, HALF), :]


def gather_lines(up_ref, own_ref, down_ref, lines_ref):
    for ref, at in ((up_ref, 0), (down_ref, (RAD + ROWS) * LINES)):
        for half in range(2):
            lines_ref[at + half * LINES_ROWS : at + (half + 1) * LINES_ROWS, :] = ref[
                RAD * COLS : RAD * COLS + LINES_ROWS, half * COLS : (half + 1) * COLS
            ].astype(jnp.float32)
    lines_ref[RAD * LINES : (RAD + ROWS) * LINES, :] = own_ref[: ROWS * LINES, :]


def own_mask():
    n = lax.broadcasted_iota(jnp.int32, (COLS, COLS), 0)
    i = lax.broadcasted_iota(jnp.int32, (COLS, COLS), 1)
    return ((i >= HALF) & (i > n)) | ((i < HALF) & (i <= n))


def fill_bands(inner_ref, outer_ref, lines_ref, inner_mask, outer_mask, l):
    for k in range(NK):
        for s in range(NR):
            at = LINES * (l + s) + NK * (NR - 1 - s) + k
            row = jnp.broadcast_to(lines_ref[pl.ds(at, 1), :], (16, COLS))
            base = pltpu.roll(row, 0, 1, stride=1, stride_axis=0).astype(jnp.bfloat16)
            for g in range(COLS // 16):
                tile = base if g == 0 else pltpu.roll(base, 16 * g, 1)
                rows = slice(k * COLS + 16 * g, k * COLS + 16 * (g + 1))
                cols = slice(s * COLS, (s + 1) * COLS)
                inner_ref[rows, cols] = tile * inner_mask[16 * g : 16 * (g + 1), :]
                outer_ref[rows, cols] = tile * outer_mask[16 * g : 16 * (g + 1), :]


def inner_kernel(
    up_ref, own_ref, down_ref, lines_own, part_ref, outer_ref, lines, cells, bands
):
    gather_lines(up_ref, lines_own, down_ref, lines)
    for row, one in enumerate(rows_in_reach(up_ref, own_ref, down_ref)):
        cells[row * COLS : row * COLS + HALF, :] = one[HALF:]
        cells[row * COLS + HALF : (row + 1) * COLS, :] = one[:HALF]
    mask = own_mask().astype(jnp.float32)
    inner_mask, outer_mask = mask.astype(jnp.bfloat16), (1.0 - mask).astype(jnp.bfloat16)
    for l in range(ROWS):
        band = bands.at[l % 2]
        fill_bands(band, outer_ref.at[l], lines, inner_mask, outer_mask, l)
        part_ref[l] = jnp.dot(
            band[...],
            cells[l * COLS : (l + NR) * COLS, :],
            preferred_element_type=jnp.float32,
        )


def outer_kernel(
    scale, bands, across, beside, part_ref, field_t, mixing, grad_ref, gw_ref, cells, spreads
):
    first = pl.multiple_of(lax.axis_index("core") * HALF, HALF)
    other = pl.multiple_of(HALF - first, HALF)
    for row in range(EXT):
        cells[pl.ds(row * COLS + first, HALF), :] = across[row]
        cells[pl.ds(row * COLS + other, HALF), :] = beside[row]
    for l in range(ROWS):
        window = cells[l * COLS : (l + NR) * COLS, :]
        for k in range(NK):
            rows = slice(k * COLS, (k + 1) * COLS)
            spread = part_ref[l, rows, :] + jnp.dot(
                bands[l, rows, :], window, preferred_element_type=jnp.float32
            )
            high = spread.astype(jnp.bfloat16)
            low = (spread - high.astype(jnp.float32)).astype(jnp.bfloat16)
            at = slice(k * CH, (k + 1) * CH)
            spreads[l * COLS : (l + 1) * COLS, at] = high
            spreads[(ROWS + l) * COLS : (ROWS + l + 1) * COLS, at] = low
    total = jnp.dot(field_t[...], spreads[...], preferred_element_type=jnp.float32) * scale
    for k in range(NK):
        gw_ref[k * CH : (k + 1) * CH, :] = total[:, k * CH : (k + 1) * CH].astype(jnp.bfloat16)
    grad = jnp.dot(spreads[: ROWS * COLS, :], mixing[...], preferred_element_type=jnp.float32)
    for l in range(ROWS):
        grad_ref[l] = grad[l * COLS : (l + 1) * COLS, :]


def exchange(x, axes):
    return lax.all_to_all(x, axes, 0, 0, tiled=True)


def per_device(field, cotangent, kernel_values, bounds, weight):
    sizes = {a: lax.axis_size(a) for a in LAT_AXES + LON_AXES}
    lat_count = math.prod(sizes[a] for a in LAT_AXES)
    lon_count = math.prod(sizes[a] for a in LON_AXES)
    params = pltpu.CompilerParams(vmem_limit_bytes=VMEM_LIMIT)
    hbm = pl.BlockSpec(memory_space=pltpu.HBM)
    packed = jax.ShapeDtypeStruct((PACKED, CH), jnp.bfloat16)
    up_own, down_own, lines_own = pl.pallas_call(
        prep_kernel,
        out_shape=(packed, packed, jax.ShapeDtypeStruct((192, COLS), jnp.float32)),
        in_specs=[hbm, hbm, hbm],
        scratch_shapes=[
            pltpu.SMEM((ROWS, 2, NR), jnp.int32),
            pltpu.VMEM((ROWS, NR, NK, COLS), jnp.float32),
            pltpu.VMEM((192, COLS), jnp.float32),
            pltpu.SemaphoreType.DMA((4,)),
        ],
        compiler_params=pltpu.CompilerParams(vmem_limit_bytes=60 * 1024 * 1024),
        name="prep",
    )(
        jnp.transpose(bounds, (1, 0, 2)),
        jnp.transpose(kernel_values, (1, 2, 0, 3)),
        cotangent.reshape(ROWS * COLS, CH),
    )
    own, lines_own, field_t, mixing = pl.pallas_call(
        own_kernel,
        out_shape=(
            jax.ShapeDtypeStruct(cotangent.shape, jnp.bfloat16),
            jax.ShapeDtypeStruct(lines_own.shape, jnp.float32),
            jax.ShapeDtypeStruct((CH, 2 * ROWS * COLS), jnp.bfloat16),
            jax.ShapeDtypeStruct((NK * CH, CH), jnp.bfloat16),
        ),
        compiler_params=params,
        cost_estimate=pl.CostEstimate(flops=0, bytes_accessed=4 * 1024 * 1024, transcendentals=0),
        name="own",
    )(cotangent, lines_own, field.reshape(ROWS * COLS, CH), weight)
    up = shifted(up_own, LAT_AXES, 1)
    down = shifted(down_own, LAT_AXES, -1)
    up, down, own, lines_own, field_t, mixing = lax.optimization_barrier(
        (up, down, own, lines_own, field_t, mixing)
    )
    side = jax.ShapeDtypeStruct((EXT, HALF, CH), jnp.bfloat16)
    across, beside = pl.pallas_call(
        middle_kernel, out_shape=(side, side), compiler_params=params, name="middle"
    )(up, own, down)
    across = lax.ppermute(
        across, LON_AXES, [(i, (i - 1 + 2 * (i % 2)) % lon_count) for i in range(lon_count)]
    )
    beside = lax.ppermute(beside, "core", [(0, 1), (1, 0)])

    cells = pltpu.VMEM((EXT * COLS, CH), jnp.bfloat16)
    band_flops = 2 * ROWS * NK * COLS * NR * COLS * CH
    part, bands = pl.pallas_call(
        inner_kernel,
        out_shape=(
            jax.ShapeDtypeStruct((ROWS, NK * COLS, CH), jnp.float32),
            jax.ShapeDtypeStruct((ROWS, NK * COLS, NR * COLS), jnp.bfloat16),
        ),
        scratch_shapes=[
            pltpu.VMEM((EXT * LINES, COLS), jnp.float32),
            cells,
            pltpu.VMEM((2, NK * COLS, NR * COLS), jnp.bfloat16),
        ],
        compiler_params=params,
        cost_estimate=pl.CostEstimate(
            flops=band_flops, bytes_accessed=4 * 1024 * 1024, transcendentals=0
        ),
        name="inner_band",
    )(up, own, down, lines_own)

    scale = 1.0 / math.sqrt(ROWS * lat_count * COLS * lon_count)
    grad_field, gw = pl.pallas_call(
        functools.partial(outer_kernel, scale),
        out_shape=(
            jax.ShapeDtypeStruct((ROWS, COLS, CH), jnp.float32),
            jax.ShapeDtypeStruct((NK * CH, CH), jnp.bfloat16),
        ),
        scratch_shapes=[cells, pltpu.VMEM((2 * ROWS * COLS, NK * CH), jnp.bfloat16)],
        compiler_params=params,
        cost_estimate=pl.CostEstimate(
            flops=band_flops * 2, bytes_accessed=6 * 1024 * 1024, transcendentals=0
        ),
        name="outer_band",
    )(bands, across, beside, part, field_t, mixing)

    plane = sizes["yh"] * lon_count
    piece = gw.shape[0] // plane
    got = exchange(gw.reshape(plane, piece, CH), PLANE)
    for axes, count in (("zl", sizes["zl"]), ("zh", sizes["zh"]), (PLANE, plane)):
        mine = jnp.sum(got.astype(jnp.float32), axis=0).astype(jnp.bfloat16)
        got = exchange(jnp.broadcast_to(mine[None], (count, piece, CH)), axes)
    return (grad_field, got.reshape(NK * CH, CH).astype(jnp.float32))


def solution(mesh):
    fine = Mesh(mesh.devices.reshape(2, 4, 4, 2, 4, 2), LAT_AXES + LON_AXES)
    return jax.shard_map(
        per_device,
        mesh=fine,
        in_specs=(
            P(LAT_AXES, LON_AXES, None),
            P(LAT_AXES, LON_AXES, None),
            P(None, LAT_AXES, None, None),
            P(None, LAT_AXES, None),
            P(),
        ),
        out_specs=(P(LAT_AXES, LON_AXES, None), P()),
        check_vma=False,
    )
```

```python
import functools
import math

import jax
import jax.numpy as jnp
from jax import lax
from jax.experimental import pallas as pl
from jax.experimental.pallas import tpu as pltpu
from jax.sharding import Mesh, PartitionSpec as P

LAT_AXES = ("yh", "zh", "zl")
LON_AXES = ("yl", "x", "core")
NEAR = ("yh", "zl", "yl", "x", "core")

ROWS, COLS, CH, NK, NR, RAD, HALF = 5, 128, 256, 4, 9, 4, 64
EXT = ROWS + 2 * RAD
LINES = NK * NR
LINES_ROWS = RAD * LINES // 2
PACKED = RAD * COLS + 80
VMEM_LIMIT = 32 * 1024 * 1024


def shifted(x, axes, step):
    count = math.prod(lax.axis_size(a) for a in axes)
    pairs = [(i, i + step) for i in range(count) if 0 <= i + step < count]
    return lax.ppermute(x, axes, pairs)


def prep_kernel(
    bounds_hbm, values_hbm, cells_hbm, up_ref, down_ref, own_ref, bounds, values, lines, sems
):
    cell_rows = RAD * COLS
    copies = [
        pltpu.make_async_copy(bounds_hbm, bounds, sems.at[0]),
        pltpu.make_async_copy(values_hbm, values, sems.at[1]),
        pltpu.make_async_copy(
            cells_hbm.at[pl.ds((ROWS - RAD) * COLS, cell_rows)],
            up_ref.at[pl.ds(0, cell_rows)],
            sems.at[2],
        ),
        pltpu.make_async_copy(
            cells_hbm.at[pl.ds(0, cell_rows)], down_ref.at[pl.ds(0, cell_rows)], sems.at[3]
        ),
    ]
    for copy in copies:
        copy.start()
    copies[0].wait()
    copies[1].wait()
    offset = lax.broadcasted_iota(jnp.int32, (NK, COLS), 1) - HALF
    for l in range(ROWS):
        for r in range(NR):
            inside = (offset >= bounds[l, 0, r]) & (offset <= bounds[l, 1, r])
            at = LINES * l + NK * r
            lines[at : at + NK, :] = jnp.where(inside, values[l, r], 0.0)
    lines[ROWS * LINES :, :] = jnp.zeros((192 - ROWS * LINES, COLS), jnp.float32)
    i = lax.broadcasted_iota(jnp.int32, (COLS, COLS), 0)
    j = lax.broadcasted_iota(jnp.int32, (COLS, COLS), 1)
    flip = ((i + j == 0) | (i + j == COLS)).astype(jnp.bfloat16)
    own_ref[...] = jnp.dot(
        lines[...].astype(jnp.bfloat16), flip, preferred_element_type=jnp.float32
    )
    for ref, row in ((up_ref, ROWS - RAD), (down_ref, 0)):
        for half in range(2):
            at = LINES * row + half * LINES_ROWS
            ref[cell_rows : cell_rows + LINES_ROWS, half * COLS : (half + 1) * COLS] = own_ref[
                at : at + LINES_ROWS, :
            ].astype(jnp.bfloat16)
        ref[cell_rows + LINES_ROWS :, :] = jnp.zeros(
            (PACKED - cell_rows - LINES_ROWS, CH), jnp.bfloat16
        )
    copies[2].wait()
    copies[3].wait()


def own_kernel(cells_ref, lines_ref, field_ref, weight_ref, own_ref, lines_own, field_t, mixing):
    own_ref[...] = cells_ref[...]
    lines_own[...] = lines_ref[...]
    field_t[...] = field_ref[...].T
    for k in range(NK):
        mixing[k * CH : (k + 1) * CH, :] = weight_ref[k * CH : (k + 1) * CH, :].T


def rows_in_reach(up_ref, own_ref, down_ref):
    for n in range(RAD):
        yield up_ref[n * COLS : (n + 1) * COLS, :]
    for n in range(ROWS):
        yield own_ref[n]
    for n in range(RAD):
        yield down_ref[n * COLS : (n + 1) * COLS, :]


def middle_kernel(up_ref, own_ref, down_ref, across_ref, beside_ref):
    first = pl.multiple_of(lax.axis_index("core") * HALF, HALF)
    other = pl.multiple_of(HALF - first, HALF)
    for n in range(RAD):
        across_ref[n] = up_ref[pl.ds(n * COLS + first, HALF), :]
        beside_ref[n] = up_ref[pl.ds(n * COLS + other, HALF), :]
        across_ref[RAD + ROWS + n] = down_ref[pl.ds(n * COLS + first, HALF), :]
        beside_ref[RAD + ROWS + n] = down_ref[pl.ds(n * COLS + other, HALF), :]
    for n in range(ROWS):
        across_ref[RAD + n] = own_ref[n, pl.ds(first, HALF), :]
        beside_ref[RAD + n] = own_ref[n, pl.ds(other, HALF), :]


def gather_lines(up_ref, own_ref, down_ref, lines_ref):
    for ref, at in ((up_ref, 0), (down_ref, (RAD + ROWS) * LINES)):
        for half in range(2):
            lines_ref[at + half * LINES_ROWS : at + (half + 1) * LINES_ROWS, :] = ref[
                RAD * COLS : RAD * COLS + LINES_ROWS, half * COLS : (half + 1) * COLS
            ].astype(jnp.float32)
    lines_ref[RAD * LINES : (RAD + ROWS) * LINES, :] = own_ref[: ROWS * LINES, :]


def own_mask():
    n = lax.broadcasted_iota(jnp.int32, (COLS, COLS), 0)
    i = lax.broadcasted_iota(jnp.int32, (COLS, COLS), 1)
    return ((i >= HALF) & (i > n)) | ((i < HALF) & (i <= n))


def fill_bands(inner_ref, outer_ref, lines_ref, inner_mask, outer_mask, l):
    for k in range(NK):
        for s in range(NR):
            at = LINES * (l + s) + NK * (NR - 1 - s) + k
            row = jnp.broadcast_to(lines_ref[pl.ds(at, 1), :], (16, COLS))
            base = pltpu.roll(row, 0, 1, stride=1, stride_axis=0).astype(jnp.bfloat16)
            for g in range(COLS // 16):
                tile = base if g == 0 else pltpu.roll(base, 16 * g, 1)
                rows = slice(k * COLS + 16 * g, k * COLS + 16 * (g + 1))
                cols = slice(s * COLS, (s + 1) * COLS)
                inner_ref[rows, cols] = tile * inner_mask[16 * g : 16 * (g + 1), :]
                outer_ref[rows, cols] = tile * outer_mask[16 * g : 16 * (g + 1), :]


def inner_kernel(
    up_ref, own_ref, down_ref, lines_own, part_ref, outer_ref, lines, cells, bands
):
    gather_lines(up_ref, lines_own, down_ref, lines)
    for row, one in enumerate(rows_in_reach(up_ref, own_ref, down_ref)):
        cells[row * COLS : row * COLS + HALF, :] = one[HALF:]
        cells[row * COLS + HALF : (row + 1) * COLS, :] = one[:HALF]
    mask = own_mask().astype(jnp.float32)
    inner_mask, outer_mask = mask.astype(jnp.bfloat16), (1.0 - mask).astype(jnp.bfloat16)
    for l in range(ROWS):
        band = bands.at[l % 2]
        fill_bands(band, outer_ref.at[l], lines, inner_mask, outer_mask, l)
        part_ref[l] = jnp.dot(
            band[...],
            cells[l * COLS : (l + NR) * COLS, :],
            preferred_element_type=jnp.float32,
        )


def outer_kernel(
    scale, bands, across, beside, part_ref, field_t, mixing, grad_ref, gw_ref, cells, spreads
):
    first = pl.multiple_of(lax.axis_index("core") * HALF, HALF)
    other = pl.multiple_of(HALF - first, HALF)
    for row in range(EXT):
        cells[pl.ds(row * COLS + first, HALF), :] = across[row]
        cells[pl.ds(row * COLS + other, HALF), :] = beside[row]
    for l in range(ROWS):
        window = cells[l * COLS : (l + NR) * COLS, :]
        for k in range(NK):
            rows = slice(k * COLS, (k + 1) * COLS)
            spread = part_ref[l, rows, :] + jnp.dot(
                bands[l, rows, :], window, preferred_element_type=jnp.float32
            )
            spreads[l * COLS : (l + 1) * COLS, k * CH : (k + 1) * CH] = spread.astype(jnp.bfloat16)
    total = jnp.dot(field_t[...], spreads[...], preferred_element_type=jnp.float32) * scale
    for k in range(NK):
        gw_ref[k * CH : (k + 1) * CH, :] = total[:, k * CH : (k + 1) * CH].astype(jnp.bfloat16)
    grad = jnp.dot(spreads[...], mixing[...], preferred_element_type=jnp.float32)
    for l in range(ROWS):
        grad_ref[l] = grad[l * COLS : (l + 1) * COLS, :]


def exchange(x, axes):
    return lax.all_to_all(x, axes, 0, 0, tiled=True)


def per_device(field, cotangent, kernel_values, bounds, weight):
    sizes = {a: lax.axis_size(a) for a in LAT_AXES + LON_AXES}
    lat_count = math.prod(sizes[a] for a in LAT_AXES)
    lon_count = math.prod(sizes[a] for a in LON_AXES)
    params = pltpu.CompilerParams(vmem_limit_bytes=VMEM_LIMIT)
    hbm = pl.BlockSpec(memory_space=pltpu.HBM)
    packed = jax.ShapeDtypeStruct((PACKED, CH), jnp.bfloat16)
    up_own, down_own, lines_own = pl.pallas_call(
        prep_kernel,
        out_shape=(packed, packed, jax.ShapeDtypeStruct((192, COLS), jnp.float32)),
        in_specs=[hbm, hbm, hbm],
        scratch_shapes=[
            pltpu.SMEM((ROWS, 2, NR), jnp.int32),
            pltpu.VMEM((ROWS, NR, NK, COLS), jnp.float32),
            pltpu.VMEM((192, COLS), jnp.float32),
            pltpu.SemaphoreType.DMA((4,)),
        ],
        compiler_params=pltpu.CompilerParams(vmem_limit_bytes=60 * 1024 * 1024),
        name="prep",
    )(
        jnp.transpose(bounds, (1, 0, 2)),
        jnp.transpose(kernel_values, (1, 2, 0, 3)),
        cotangent.reshape(ROWS * COLS, CH),
    )
    own, lines_own, field_t, mixing = pl.pallas_call(
        own_kernel,
        out_shape=(
            jax.ShapeDtypeStruct(cotangent.shape, jnp.bfloat16),
            jax.ShapeDtypeStruct(lines_own.shape, jnp.float32),
            jax.ShapeDtypeStruct((CH, ROWS * COLS), jnp.bfloat16),
            jax.ShapeDtypeStruct((NK * CH, CH), jnp.bfloat16),
        ),
        compiler_params=params,
        cost_estimate=pl.CostEstimate(flops=0, bytes_accessed=4 * 1024 * 1024, transcendentals=0),
        name="own",
    )(cotangent, lines_own, field.reshape(ROWS * COLS, CH), weight)
    up = shifted(up_own, LAT_AXES, 1)
    down = shifted(down_own, LAT_AXES, -1)
    up, down, own, lines_own, field_t, mixing = lax.optimization_barrier(
        (up, down, own, lines_own, field_t, mixing)
    )
    side = jax.ShapeDtypeStruct((EXT, HALF, CH), jnp.bfloat16)
    across, beside = pl.pallas_call(
        middle_kernel, out_shape=(side, side), compiler_params=params, name="middle"
    )(up, own, down)
    across = lax.ppermute(
        across, LON_AXES, [(i, (i - 1 + 2 * (i % 2)) % lon_count) for i in range(lon_count)]
    )
    beside = lax.ppermute(beside, "core", [(0, 1), (1, 0)])

    cells = pltpu.VMEM((EXT * COLS, CH), jnp.bfloat16)
    band_flops = 2 * ROWS * NK * COLS * NR * COLS * CH
    part, bands = pl.pallas_call(
        inner_kernel,
        out_shape=(
            jax.ShapeDtypeStruct((ROWS, NK * COLS, CH), jnp.float32),
            jax.ShapeDtypeStruct((ROWS, NK * COLS, NR * COLS), jnp.bfloat16),
        ),
        scratch_shapes=[
            pltpu.VMEM((EXT * LINES, COLS), jnp.float32),
            cells,
            pltpu.VMEM((2, NK * COLS, NR * COLS), jnp.bfloat16),
        ],
        compiler_params=params,
        cost_estimate=pl.CostEstimate(
            flops=band_flops, bytes_accessed=4 * 1024 * 1024, transcendentals=0
        ),
        name="inner_band",
    )(up, own, down, lines_own)

    scale = 1.0 / math.sqrt(ROWS * lat_count * COLS * lon_count)
    grad_field, gw = pl.pallas_call(
        functools.partial(outer_kernel, scale),
        out_shape=(
            jax.ShapeDtypeStruct((ROWS, COLS, CH), jnp.float32),
            jax.ShapeDtypeStruct((NK * CH, CH), jnp.bfloat16),
        ),
        scratch_shapes=[cells, pltpu.VMEM((ROWS * COLS, NK * CH), jnp.bfloat16)],
        compiler_params=params,
        cost_estimate=pl.CostEstimate(
            flops=band_flops * 2, bytes_accessed=6 * 1024 * 1024, transcendentals=0
        ),
        name="outer_band",
    )(bands, across, beside, part, field_t, mixing)

    near = math.prod(sizes[a] for a in NEAR)
    piece = gw.shape[0] // near
    got = exchange(gw.reshape(near, piece, CH), NEAR)
    for axes, count in (("zh", sizes["zh"]), (NEAR, near)):
        mine = jnp.sum(got.astype(jnp.float32), axis=0).astype(jnp.bfloat16)
        got = exchange(jnp.broadcast_to(mine[None], (count, piece, CH)), axes)
    return (grad_field, got.reshape(NK * CH, CH).astype(jnp.float32))


def solution(mesh):
    fine = Mesh(mesh.devices.reshape(2, 8, 2, 2, 4, 2), LAT_AXES + LON_AXES)
    return jax.shard_map(
        per_device,
        mesh=fine,
        in_specs=(
            P(LAT_AXES, LON_AXES, None),
            P(LAT_AXES, LON_AXES, None),
            P(None, LAT_AXES, None, None),
            P(None, LAT_AXES, None),
            P(),
        ),
        out_specs=(P(LAT_AXES, LON_AXES, None), P()),
        check_vma=False,
    )
```

```python
import functools
import math

import jax
import jax.numpy as jnp
from jax import lax
from jax.experimental import pallas as pl
from jax.experimental.pallas import tpu as pltpu
from jax.sharding import Mesh, PartitionSpec as P

LAT_AXES = ("yh", "zh", "zl")
LON_AXES = ("yl", "x", "core")
NEAR = ("yh", "zl", "yl", "x", "core")

ROWS, COLS, CH, NK, NR, RAD, HALF = 5, 128, 256, 4, 9, 4, 64
EXT = ROWS + 2 * RAD
LINES = NK * NR
CELL_ROWS = RAD * COLS
PACK_ROWS = 32
PACKED = CELL_ROWS + PACK_ROWS
VMEM_LIMIT = 32 * 1024 * 1024


def swapped(x, axes, start):
    count = math.prod(lax.axis_size(a) for a in axes)
    pairs = [(i, i + 1) for i in range(start, count - 1, 2)]
    return lax.ppermute(x, axes, pairs + [(j, i) for i, j in pairs])


def packed_groups():
    above = [(n, NR - 1 - n + t) for n in range(RAD) for t in range(n + 1)]
    below = [(n, t) for n in range(RAD) for t in range(RAD - n)]
    for place, (one, two) in enumerate(zip(above, below)):
        half = len(above) // 2
        yield (place // half) * PACK_ROWS + (place % half) * NK, one, two


def prep_kernel(
    bounds_hbm, values_hbm, cells_hbm, far_ref, near_ref, own_ref, bounds, values, lines, wide, sems
):
    odd = lax.axis_index("zl")
    copies = [
        pltpu.make_async_copy(bounds_hbm, bounds, sems.at[0]),
        pltpu.make_async_copy(values_hbm, values, sems.at[1]),
        pltpu.make_async_copy(
            cells_hbm.at[pl.ds(pl.multiple_of(odd * COLS, COLS), CELL_ROWS)],
            far_ref.at[pl.ds(0, CELL_ROWS)],
            sems.at[2],
        ),
        pltpu.make_async_copy(
            cells_hbm.at[pl.ds(pl.multiple_of((1 - odd) * COLS, COLS), CELL_ROWS)],
            near_ref.at[pl.ds(0, CELL_ROWS)],
            sems.at[3],
        ),
    ]
    for copy in copies:
        copy.start()
    copies[0].wait()
    copies[1].wait()
    offset = lax.broadcasted_iota(jnp.int32, (NK, COLS), 1) - HALF
    for l in range(ROWS):
        for r in range(NR):
            inside = (offset >= bounds[l, 0, r]) & (offset <= bounds[l, 1, r])
            at = LINES * l + NK * r
            lines[at : at + NK, :] = jnp.where(inside, values[l, r], 0.0)
    lines[ROWS * LINES :, :] = jnp.zeros((192 - ROWS * LINES, COLS), jnp.float32)
    i = lax.broadcasted_iota(jnp.int32, (COLS, COLS), 0)
    j = lax.broadcasted_iota(jnp.int32, (COLS, COLS), 1)
    flip = ((i + j == 0) | (i + j == COLS)).astype(jnp.bfloat16)
    own_ref[...] = jnp.dot(
        lines[...].astype(jnp.bfloat16), flip, preferred_element_type=jnp.float32
    )
    wide[...] = jnp.zeros(wide.shape, jnp.float32)
    for place, above, below in packed_groups():
        for side, (row, r) in enumerate(((ROWS - RAD + above[0], above[1]), below)):
            at = LINES * row + NK * r
            wide[side, place : place + NK, :] = own_ref[at : at + NK, :]
    for side, ref in ((1 - odd, far_ref), (odd, near_ref)):
        for half in range(2):
            ref[CELL_ROWS:, half * COLS : (half + 1) * COLS] = wide[
                side, half * PACK_ROWS : (half + 1) * PACK_ROWS, :
            ].astype(jnp.bfloat16)
    copies[2].wait()
    copies[3].wait()


def own_kernel(cells_ref, lines_ref, field_ref, weight_ref, own_ref, lines_own, field_t, mixing):
    own_ref[...] = cells_ref[...]
    lines_own[...] = lines_ref[...]
    field_t[...] = field_ref[...].T
    for k in range(NK):
        mixing[k * CH : (k + 1) * CH, :] = weight_ref[k * CH : (k + 1) * CH, :].T


def rows_in_reach(up_ref, own_ref, down_ref):
    for n in range(RAD):
        yield up_ref[n * COLS : (n + 1) * COLS, :]
    for n in range(ROWS):
        yield own_ref[n]
    for n in range(RAD):
        yield down_ref[n * COLS : (n + 1) * COLS, :]


def by_parity(far_ref, near_ref, body):
    odd = lax.axis_index("zl")

    @pl.when(odd == 0)
    def _():
        body(far_ref, near_ref)

    @pl.when(odd == 1)
    def _():
        body(near_ref, far_ref)


def middle_kernel(far_ref, own_ref, near_ref, across_ref, beside_ref):
    first = pl.multiple_of(lax.axis_index("core") * HALF, HALF)
    other = pl.multiple_of(HALF - first, HALF)

    def halo(up_ref, down_ref):
        for n in range(RAD):
            across_ref[n] = up_ref[pl.ds(n * COLS + first, HALF), :]
            beside_ref[n] = up_ref[pl.ds(n * COLS + other, HALF), :]
            across_ref[RAD + ROWS + n] = down_ref[pl.ds(n * COLS + first, HALF), :]
            beside_ref[RAD + ROWS + n] = down_ref[pl.ds(n * COLS + other, HALF), :]

    by_parity(far_ref, near_ref, halo)
    for n in range(ROWS):
        across_ref[RAD + n] = own_ref[n, pl.ds(first, HALF), :]
        beside_ref[RAD + n] = own_ref[n, pl.ds(other, HALF), :]


def gather_lines(up_ref, own_ref, down_ref, lines_ref, wide):
    for side, ref in enumerate((up_ref, down_ref)):
        for half in range(2):
            wide[side, half * PACK_ROWS : (half + 1) * PACK_ROWS, :] = ref[
                CELL_ROWS:, half * COLS : (half + 1) * COLS
            ].astype(jnp.float32)
    for place, above, below in packed_groups():
        for side, (row, r) in enumerate((above, (RAD + ROWS + below[0], below[1]))):
            at = LINES * row + NK * r
            lines_ref[at : at + NK, :] = wide[side, place : place + NK, :]
    lines_ref[RAD * LINES : (RAD + ROWS) * LINES, :] = own_ref[: ROWS * LINES, :]


def own_mask():
    n = lax.broadcasted_iota(jnp.int32, (COLS, COLS), 0)
    i = lax.broadcasted_iota(jnp.int32, (COLS, COLS), 1)
    return ((i >= HALF) & (i > n)) | ((i < HALF) & (i <= n))


def fill_bands(inner_ref, outer_ref, lines_ref, inner_mask, outer_mask, l):
    for k in range(NK):
        for s in range(NR):
            at = LINES * (l + s) + NK * (NR - 1 - s) + k
            row = jnp.broadcast_to(lines_ref[pl.ds(at, 1), :], (16, COLS))
            base = pltpu.roll(row, 0, 1, stride=1, stride_axis=0).astype(jnp.bfloat16)
            for g in range(COLS // 16):
                tile = base if g == 0 else pltpu.roll(base, 16 * g, 1)
                rows = slice(k * COLS + 16 * g, k * COLS + 16 * (g + 1))
                cols = slice(s * COLS, (s + 1) * COLS)
                inner_ref[rows, cols] = tile * inner_mask[16 * g : 16 * (g + 1), :]
                outer_ref[rows, cols] = tile * outer_mask[16 * g : 16 * (g + 1), :]


def inner_kernel(
    far_ref, own_ref, near_ref, lines_own, part_ref, outer_ref, lines, wide, cells, bands
):
    def load(up_ref, down_ref):
        gather_lines(up_ref, lines_own, down_ref, lines, wide)
        for row, one in enumerate(rows_in_reach(up_ref, own_ref, down_ref)):
            cells[row * COLS : row * COLS + HALF, :] = one[HALF:]
            cells[row * COLS + HALF : (row + 1) * COLS, :] = one[:HALF]

    by_parity(far_ref, near_ref, load)
    mask = own_mask().astype(jnp.float32)
    inner_mask, outer_mask = mask.astype(jnp.bfloat16), (1.0 - mask).astype(jnp.bfloat16)
    for l in range(ROWS):
        band = bands.at[l % 2]
        fill_bands(band, outer_ref.at[l], lines, inner_mask, outer_mask, l)
        part_ref[l] = jnp.dot(
            band[...],
            cells[l * COLS : (l + NR) * COLS, :],
            preferred_element_type=jnp.float32,
        )


def outer_kernel(
    scale, bands, across, beside, part_ref, field_t, mixing, grad_ref, gw_ref, cells, spreads
):
    first = pl.multiple_of(lax.axis_index("core") * HALF, HALF)
    other = pl.multiple_of(HALF - first, HALF)
    for row in range(EXT):
        cells[pl.ds(row * COLS + first, HALF), :] = across[row]
        cells[pl.ds(row * COLS + other, HALF), :] = beside[row]
    for l in range(ROWS):
        window = cells[l * COLS : (l + NR) * COLS, :]
        for k in range(NK):
            rows = slice(k * COLS, (k + 1) * COLS)
            spread = part_ref[l, rows, :] + jnp.dot(
                bands[l, rows, :], window, preferred_element_type=jnp.float32
            )
            spreads[l * COLS : (l + 1) * COLS, k * CH : (k + 1) * CH] = spread.astype(jnp.bfloat16)
    total = jnp.dot(field_t[...], spreads[...], preferred_element_type=jnp.float32) * scale
    for k in range(NK):
        gw_ref[k * CH : (k + 1) * CH, :] = total[:, k * CH : (k + 1) * CH].astype(jnp.bfloat16)
    grad = jnp.dot(spreads[...], mixing[...], preferred_element_type=jnp.float32)
    for l in range(ROWS):
        grad_ref[l] = grad[l * COLS : (l + 1) * COLS, :]


def exchange(x, axes):
    return lax.all_to_all(x, axes, 0, 0, tiled=True)


def per_device(field, cotangent, kernel_values, bounds, weight):
    sizes = {a: lax.axis_size(a) for a in LAT_AXES + LON_AXES}
    lat_count = math.prod(sizes[a] for a in LAT_AXES)
    lon_count = math.prod(sizes[a] for a in LON_AXES)
    params = pltpu.CompilerParams(vmem_limit_bytes=VMEM_LIMIT)
    hbm = pl.BlockSpec(memory_space=pltpu.HBM)
    wide = pltpu.VMEM((2, 2 * PACK_ROWS, COLS), jnp.float32)
    packed = jax.ShapeDtypeStruct((PACKED, CH), jnp.bfloat16)
    far, near, lines_own = pl.pallas_call(
        prep_kernel,
        out_shape=(packed, packed, jax.ShapeDtypeStruct((192, COLS), jnp.float32)),
        in_specs=[hbm, hbm, hbm],
        scratch_shapes=[
            pltpu.SMEM((ROWS, 2, NR), jnp.int32),
            pltpu.VMEM((ROWS, NR, NK, COLS), jnp.float32),
            pltpu.VMEM((192, COLS), jnp.float32),
            wide,
            pltpu.SemaphoreType.DMA((4,)),
        ],
        compiler_params=pltpu.CompilerParams(vmem_limit_bytes=60 * 1024 * 1024),
        name="prep",
    )(
        jnp.transpose(bounds, (1, 0, 2)),
        jnp.transpose(kernel_values, (1, 2, 0, 3)),
        cotangent.reshape(ROWS * COLS, CH),
    )
    own, lines_own, field_t, mixing = pl.pallas_call(
        own_kernel,
        out_shape=(
            jax.ShapeDtypeStruct(cotangent.shape, jnp.bfloat16),
            jax.ShapeDtypeStruct(lines_own.shape, jnp.float32),
            jax.ShapeDtypeStruct((CH, ROWS * COLS), jnp.bfloat16),
            jax.ShapeDtypeStruct((NK * CH, CH), jnp.bfloat16),
        ),
        compiler_params=params,
        cost_estimate=pl.CostEstimate(flops=0, bytes_accessed=4 * 1024 * 1024, transcendentals=0),
        name="own",
    )(cotangent, lines_own, field.reshape(ROWS * COLS, CH), weight)
    far = swapped(far, LAT_AXES, 1)
    near = swapped(near, LAT_AXES, 0)
    far, near, own, lines_own, field_t, mixing = lax.optimization_barrier(
        (far, near, own, lines_own, field_t, mixing)
    )
    side = jax.ShapeDtypeStruct((EXT, HALF, CH), jnp.bfloat16)
    across, beside = pl.pallas_call(
        middle_kernel, out_shape=(side, side), compiler_params=params, name="middle"
    )(far, own, near)
    across = lax.ppermute(
        across, LON_AXES, [(i, (i - 1 + 2 * (i % 2)) % lon_count) for i in range(lon_count)]
    )
    beside = lax.ppermute(beside, "core", [(0, 1), (1, 0)])

    cells = pltpu.VMEM((EXT * COLS, CH), jnp.bfloat16)
    band_flops = 2 * ROWS * NK * COLS * NR * COLS * CH
    part, bands = pl.pallas_call(
        inner_kernel,
        out_shape=(
            jax.ShapeDtypeStruct((ROWS, NK * COLS, CH), jnp.float32),
            jax.ShapeDtypeStruct((ROWS, NK * COLS, NR * COLS), jnp.bfloat16),
        ),
        scratch_shapes=[
            pltpu.VMEM((EXT * LINES, COLS), jnp.float32),
            wide,
            cells,
            pltpu.VMEM((2, NK * COLS, NR * COLS), jnp.bfloat16),
        ],
        compiler_params=params,
        cost_estimate=pl.CostEstimate(
            flops=band_flops, bytes_accessed=4 * 1024 * 1024, transcendentals=0
        ),
        name="inner_band",
    )(far, own, near, lines_own)

    scale = 1.0 / math.sqrt(ROWS * lat_count * COLS * lon_count)
    grad_field, gw = pl.pallas_call(
        functools.partial(outer_kernel, scale),
        out_shape=(
            jax.ShapeDtypeStruct((ROWS, COLS, CH), jnp.float32),
            jax.ShapeDtypeStruct((NK * CH, CH), jnp.bfloat16),
        ),
        scratch_shapes=[cells, pltpu.VMEM((ROWS * COLS, NK * CH), jnp.bfloat16)],
        compiler_params=params,
        cost_estimate=pl.CostEstimate(
            flops=band_flops * 2, bytes_accessed=6 * 1024 * 1024, transcendentals=0
        ),
        name="outer_band",
    )(bands, across, beside, part, field_t, mixing)

    near = math.prod(sizes[a] for a in NEAR)
    piece = gw.shape[0] // near
    got = exchange(gw.reshape(near, piece, CH), NEAR)
    for axes, count in (("zh", sizes["zh"]), (NEAR, near)):
        mine = jnp.sum(got.astype(jnp.float32), axis=0).astype(jnp.bfloat16)
        got = exchange(jnp.broadcast_to(mine[None], (count, piece, CH)), axes)
    return (grad_field, got.reshape(NK * CH, CH).astype(jnp.float32))


def solution(mesh):
    fine = Mesh(mesh.devices.reshape(2, 8, 2, 2, 4, 2), LAT_AXES + LON_AXES)
    return jax.shard_map(
        per_device,
        mesh=fine,
        in_specs=(
            P(LAT_AXES, LON_AXES, None),
            P(LAT_AXES, LON_AXES, None),
            P(None, LAT_AXES, None, None),
            P(None, LAT_AXES, None),
            P(),
        ),
        out_specs=(P(LAT_AXES, LON_AXES, None), P()),
        check_vma=False,
    )
```

```python
import functools
import math

import jax
import jax.numpy as jnp
from jax import lax
from jax.experimental import pallas as pl
from jax.experimental.pallas import tpu as pltpu
from jax.sharding import Mesh, PartitionSpec as P

LAT_AXES = ("yh", "z3", "z2", "z1", "zl")
LON_AXES = ("yl", "x", "core")
DEPTH = ("z1", "z2", "z3")
NEAR = ("yh", "zl", "yl", "x", "core")

ROWS, COLS, CH, NK, NR, RAD, HALF = 5, 128, 256, 4, 9, 4, 64
EXT = ROWS + 2 * RAD
LINES = NK * NR
CELL_ROWS = RAD * COLS
PACK_ROWS = 32
PACKED = CELL_ROWS + PACK_ROWS
VMEM_LIMIT = 32 * 1024 * 1024


def swapped(x, axes, start):
    count = math.prod(lax.axis_size(a) for a in axes)
    pairs = [(i, i + 1) for i in range(start, count - 1, 2)]
    return lax.ppermute(x, axes, pairs + [(j, i) for i, j in pairs])


def packed_groups():
    above = [(n, NR - 1 - n + t) for n in range(RAD) for t in range(n + 1)]
    below = [(n, t) for n in range(RAD) for t in range(RAD - n)]
    for place, (one, two) in enumerate(zip(above, below)):
        half = len(above) // 2
        yield (place // half) * PACK_ROWS + (place % half) * NK, one, two


def prep_kernel(
    bounds_hbm, values_hbm, cells_hbm, far_ref, near_ref, own_ref, bounds, values, lines, wide, sems
):
    odd = lax.axis_index("zl")
    copies = [
        pltpu.make_async_copy(bounds_hbm, bounds, sems.at[0]),
        pltpu.make_async_copy(values_hbm, values, sems.at[1]),
        pltpu.make_async_copy(
            cells_hbm.at[pl.ds(pl.multiple_of(odd * COLS, COLS), CELL_ROWS)],
            far_ref.at[pl.ds(0, CELL_ROWS)],
            sems.at[2],
        ),
        pltpu.make_async_copy(
            cells_hbm.at[pl.ds(pl.multiple_of((1 - odd) * COLS, COLS), CELL_ROWS)],
            near_ref.at[pl.ds(0, CELL_ROWS)],
            sems.at[3],
        ),
    ]
    for copy in copies:
        copy.start()
    copies[0].wait()
    copies[1].wait()
    offset = lax.broadcasted_iota(jnp.int32, (NK, COLS), 1) - HALF
    for l in range(ROWS):
        for r in range(NR):
            inside = (offset >= bounds[l, 0, r]) & (offset <= bounds[l, 1, r])
            at = LINES * l + NK * r
            lines[at : at + NK, :] = jnp.where(inside, values[l, r], 0.0)
    lines[ROWS * LINES :, :] = jnp.zeros((192 - ROWS * LINES, COLS), jnp.float32)
    i = lax.broadcasted_iota(jnp.int32, (COLS, COLS), 0)
    j = lax.broadcasted_iota(jnp.int32, (COLS, COLS), 1)
    flip = ((i + j == 0) | (i + j == COLS)).astype(jnp.bfloat16)
    own_ref[...] = jnp.dot(
        lines[...].astype(jnp.bfloat16), flip, preferred_element_type=jnp.float32
    )
    wide[...] = jnp.zeros(wide.shape, jnp.float32)
    for place, above, below in packed_groups():
        for side, (row, r) in enumerate(((ROWS - RAD + above[0], above[1]), below)):
            at = LINES * row + NK * r
            wide[side, place : place + NK, :] = own_ref[at : at + NK, :]
    for side, ref in ((1 - odd, far_ref), (odd, near_ref)):
        for half in range(2):
            ref[CELL_ROWS:, half * COLS : (half + 1) * COLS] = wide[
                side, half * PACK_ROWS : (half + 1) * PACK_ROWS, :
            ].astype(jnp.bfloat16)
    copies[2].wait()
    copies[3].wait()


def own_kernel(cells_ref, lines_ref, field_ref, weight_ref, own_ref, lines_own, field_t, mixing):
    own_ref[...] = cells_ref[...]
    lines_own[...] = lines_ref[...]
    field_t[...] = field_ref[...].T
    for k in range(NK):
        mixing[k * CH : (k + 1) * CH, :] = weight_ref[k * CH : (k + 1) * CH, :].T


def rows_in_reach(up_ref, own_ref, down_ref):
    for n in range(RAD):
        yield up_ref[n * COLS : (n + 1) * COLS, :]
    for n in range(ROWS):
        yield own_ref[n]
    for n in range(RAD):
        yield down_ref[n * COLS : (n + 1) * COLS, :]


def by_parity(far_ref, near_ref, body):
    odd = lax.axis_index("zl")

    @pl.when(odd == 0)
    def _():
        body(far_ref, near_ref)

    @pl.when(odd == 1)
    def _():
        body(near_ref, far_ref)


def middle_kernel(far_ref, own_ref, near_ref, across_ref, beside_ref):
    first = pl.multiple_of(lax.axis_index("core") * HALF, HALF)
    other = pl.multiple_of(HALF - first, HALF)

    def halo(up_ref, down_ref):
        for n in range(RAD):
            across_ref[n] = up_ref[pl.ds(n * COLS + first, HALF), :]
            beside_ref[n] = up_ref[pl.ds(n * COLS + other, HALF), :]
            across_ref[RAD + ROWS + n] = down_ref[pl.ds(n * COLS + first, HALF), :]
            beside_ref[RAD + ROWS + n] = down_ref[pl.ds(n * COLS + other, HALF), :]

    by_parity(far_ref, near_ref, halo)
    for n in range(ROWS):
        across_ref[RAD + n] = own_ref[n, pl.ds(first, HALF), :]
        beside_ref[RAD + n] = own_ref[n, pl.ds(other, HALF), :]


def gather_lines(up_ref, own_ref, down_ref, lines_ref, wide):
    for side, ref in enumerate((up_ref, down_ref)):
        for half in range(2):
            wide[side, half * PACK_ROWS : (half + 1) * PACK_ROWS, :] = ref[
                CELL_ROWS:, half * COLS : (half + 1) * COLS
            ].astype(jnp.float32)
    for place, above, below in packed_groups():
        for side, (row, r) in enumerate((above, (RAD + ROWS + below[0], below[1]))):
            at = LINES * row + NK * r
            lines_ref[at : at + NK, :] = wide[side, place : place + NK, :]
    lines_ref[RAD * LINES : (RAD + ROWS) * LINES, :] = own_ref[: ROWS * LINES, :]


def own_mask():
    n = lax.broadcasted_iota(jnp.int32, (COLS, COLS), 0)
    i = lax.broadcasted_iota(jnp.int32, (COLS, COLS), 1)
    return ((i >= HALF) & (i > n)) | ((i < HALF) & (i <= n))


def fill_bands(inner_ref, outer_ref, lines_ref, inner_mask, outer_mask, l):
    for k in range(NK):
        for s in range(NR):
            at = LINES * (l + s) + NK * (NR - 1 - s) + k
            row = jnp.broadcast_to(lines_ref[pl.ds(at, 1), :], (16, COLS))
            base = pltpu.roll(row, 0, 1, stride=1, stride_axis=0).astype(jnp.bfloat16)
            for g in range(COLS // 16):
                tile = base if g == 0 else pltpu.roll(base, 16 * g, 1)
                rows = slice(k * COLS + 16 * g, k * COLS + 16 * (g + 1))
                cols = slice(s * COLS, (s + 1) * COLS)
                inner_ref[rows, cols] = tile * inner_mask[16 * g : 16 * (g + 1), :]
                outer_ref[rows, cols] = tile * outer_mask[16 * g : 16 * (g + 1), :]


def inner_kernel(
    far_ref, own_ref, near_ref, lines_own, part_ref, outer_ref, lines, wide, cells, bands
):
    def load(up_ref, down_ref):
        gather_lines(up_ref, lines_own, down_ref, lines, wide)
        for row, one in enumerate(rows_in_reach(up_ref, own_ref, down_ref)):
            cells[row * COLS : row * COLS + HALF, :] = one[HALF:]
            cells[row * COLS + HALF : (row + 1) * COLS, :] = one[:HALF]

    by_parity(far_ref, near_ref, load)
    mask = own_mask().astype(jnp.float32)
    inner_mask, outer_mask = mask.astype(jnp.bfloat16), (1.0 - mask).astype(jnp.bfloat16)
    for l in range(ROWS):
        band = bands.at[l % 2]
        fill_bands(band, outer_ref.at[l], lines, inner_mask, outer_mask, l)
        part_ref[l] = jnp.dot(
            band[...],
            cells[l * COLS : (l + NR) * COLS, :],
            preferred_element_type=jnp.float32,
        )


def outer_kernel(
    scale, bands, across, beside, part_ref, field_t, mixing, grad_ref, gw_ref, cells, spreads
):
    first = pl.multiple_of(lax.axis_index("core") * HALF, HALF)
    other = pl.multiple_of(HALF - first, HALF)
    for row in range(EXT):
        cells[pl.ds(row * COLS + first, HALF), :] = across[row]
        cells[pl.ds(row * COLS + other, HALF), :] = beside[row]
    for l in range(ROWS):
        window = cells[l * COLS : (l + NR) * COLS, :]
        for k in range(NK):
            rows = slice(k * COLS, (k + 1) * COLS)
            spread = part_ref[l, rows, :] + jnp.dot(
                bands[l, rows, :], window, preferred_element_type=jnp.float32
            )
            spreads[l * COLS : (l + 1) * COLS, k * CH : (k + 1) * CH] = spread.astype(jnp.bfloat16)
    total = jnp.dot(field_t[...], spreads[...], preferred_element_type=jnp.float32) * scale
    for k in range(NK):
        gw_ref[k * CH : (k + 1) * CH, :] = total[:, k * CH : (k + 1) * CH].astype(jnp.bfloat16)
    grad = jnp.dot(spreads[...], mixing[...], preferred_element_type=jnp.float32)
    for l in range(ROWS):
        grad_ref[l] = grad[l * COLS : (l + 1) * COLS, :]


def exchange(x, axes):
    return lax.all_to_all(x, axes, 0, 0, tiled=True)


def per_device(field, cotangent, kernel_values, bounds, weight):
    sizes = {a: lax.axis_size(a) for a in LAT_AXES + LON_AXES}
    lat_count = math.prod(sizes[a] for a in LAT_AXES)
    lon_count = math.prod(sizes[a] for a in LON_AXES)
    params = pltpu.CompilerParams(vmem_limit_bytes=VMEM_LIMIT)
    hbm = pl.BlockSpec(memory_space=pltpu.HBM)
    wide = pltpu.VMEM((2, 2 * PACK_ROWS, COLS), jnp.float32)
    packed = jax.ShapeDtypeStruct((PACKED, CH), jnp.bfloat16)
    far, near, lines_own = pl.pallas_call(
        prep_kernel,
        out_shape=(packed, packed, jax.ShapeDtypeStruct((192, COLS), jnp.float32)),
        in_specs=[hbm, hbm, hbm],
        scratch_shapes=[
            pltpu.SMEM((ROWS, 2, NR), jnp.int32),
            pltpu.VMEM((ROWS, NR, NK, COLS), jnp.float32),
            pltpu.VMEM((192, COLS), jnp.float32),
            wide,
            pltpu.SemaphoreType.DMA((4,)),
        ],
        compiler_params=pltpu.CompilerParams(vmem_limit_bytes=60 * 1024 * 1024),
        name="prep",
    )(
        jnp.transpose(bounds, (1, 0, 2)),
        jnp.transpose(kernel_values, (1, 2, 0, 3)),
        cotangent.reshape(ROWS * COLS, CH),
    )
    own, lines_own, field_t, mixing = pl.pallas_call(
        own_kernel,
        out_shape=(
            jax.ShapeDtypeStruct(cotangent.shape, jnp.bfloat16),
            jax.ShapeDtypeStruct(lines_own.shape, jnp.float32),
            jax.ShapeDtypeStruct((CH, ROWS * COLS), jnp.bfloat16),
            jax.ShapeDtypeStruct((NK * CH, CH), jnp.bfloat16),
        ),
        compiler_params=params,
        cost_estimate=pl.CostEstimate(flops=0, bytes_accessed=4 * 1024 * 1024, transcendentals=0),
        name="own",
    )(cotangent, lines_own, field.reshape(ROWS * COLS, CH), weight)
    far = swapped(far, LAT_AXES, 1)
    near = swapped(near, LAT_AXES, 0)
    far, near, own, lines_own, field_t, mixing = lax.optimization_barrier(
        (far, near, own, lines_own, field_t, mixing)
    )
    side = jax.ShapeDtypeStruct((EXT, HALF, CH), jnp.bfloat16)
    across, beside = pl.pallas_call(
        middle_kernel, out_shape=(side, side), compiler_params=params, name="middle"
    )(far, own, near)
    across = lax.ppermute(
        across, LON_AXES, [(i, (i - 1 + 2 * (i % 2)) % lon_count) for i in range(lon_count)]
    )
    beside = lax.ppermute(beside, "core", [(0, 1), (1, 0)])

    cells = pltpu.VMEM((EXT * COLS, CH), jnp.bfloat16)
    band_flops = 2 * ROWS * NK * COLS * NR * COLS * CH
    part, bands = pl.pallas_call(
        inner_kernel,
        out_shape=(
            jax.ShapeDtypeStruct((ROWS, NK * COLS, CH), jnp.float32),
            jax.ShapeDtypeStruct((ROWS, NK * COLS, NR * COLS), jnp.bfloat16),
        ),
        scratch_shapes=[
            pltpu.VMEM((EXT * LINES, COLS), jnp.float32),
            wide,
            cells,
            pltpu.VMEM((2, NK * COLS, NR * COLS), jnp.bfloat16),
        ],
        compiler_params=params,
        cost_estimate=pl.CostEstimate(
            flops=band_flops, bytes_accessed=4 * 1024 * 1024, transcendentals=0
        ),
        name="inner_band",
    )(far, own, near, lines_own)

    scale = 1.0 / math.sqrt(ROWS * lat_count * COLS * lon_count)
    grad_field, gw = pl.pallas_call(
        functools.partial(outer_kernel, scale),
        out_shape=(
            jax.ShapeDtypeStruct((ROWS, COLS, CH), jnp.float32),
            jax.ShapeDtypeStruct((NK * CH, CH), jnp.bfloat16),
        ),
        scratch_shapes=[cells, pltpu.VMEM((ROWS * COLS, NK * CH), jnp.bfloat16)],
        compiler_params=params,
        cost_estimate=pl.CostEstimate(
            flops=band_flops * 2, bytes_accessed=6 * 1024 * 1024, transcendentals=0
        ),
        name="outer_band",
    )(bands, across, beside, part, field_t, mixing)

    near = math.prod(sizes[a] for a in NEAR)
    piece = gw.shape[0] // near
    got = exchange(gw.reshape(near, piece, CH), NEAR)
    for axes, count in ((DEPTH, math.prod(sizes[a] for a in DEPTH)), (NEAR, near)):
        mine = jnp.sum(got.astype(jnp.float32), axis=0).astype(jnp.bfloat16)
        got = exchange(jnp.broadcast_to(mine[None], (count, piece, CH)), axes)
    return (grad_field, got.reshape(NK * CH, CH).astype(jnp.float32))


def solution(mesh):
    fine = Mesh(mesh.devices.reshape(2, 2, 2, 2, 2, 2, 4, 2), LAT_AXES + LON_AXES)
    return jax.shard_map(
        per_device,
        mesh=fine,
        in_specs=(
            P(LAT_AXES, LON_AXES, None),
            P(LAT_AXES, LON_AXES, None),
            P(None, LAT_AXES, None, None),
            P(None, LAT_AXES, None),
            P(),
        ),
        out_specs=(P(LAT_AXES, LON_AXES, None), P()),
        check_vma=False,
    )
```

```python
import functools
import math

import jax
import jax.numpy as jnp
from jax import lax
from jax.experimental import pallas as pl
from jax.experimental.pallas import tpu as pltpu
from jax.sharding import Mesh, PartitionSpec as P

LAT_AXES = ("yh", "z3", "z2", "z1", "zl")
LON_AXES = ("yl", "x", "core")
DEPTH = ("z1", "z2", "z3")
NEAR = ("yh", "zl", "yl", "x", "core")

ROWS, COLS, CH, NK, NR, RAD, HALF = 5, 128, 256, 4, 9, 4, 64
EXT = ROWS + 2 * RAD
LINES = NK * NR
CELL_ROWS = RAD * COLS
PACK_ROWS = 32
PACKED = CELL_ROWS + PACK_ROWS
VMEM_LIMIT = 32 * 1024 * 1024


def swapped(x, axes, start):
    count = math.prod(lax.axis_size(a) for a in axes)
    pairs = [(i, i + 1) for i in range(start, count - 1, 2)]
    return lax.ppermute(x, axes, pairs + [(j, i) for i, j in pairs])


def packed_groups():
    above = [(n, NR - 1 - n + t) for n in range(RAD) for t in range(n + 1)]
    below = [(n, t) for n in range(RAD) for t in range(RAD - n)]
    for place, (one, two) in enumerate(zip(above, below)):
        half = len(above) // 2
        yield (place // half) * PACK_ROWS + (place % half) * NK, one, two


def prep_kernel(
    bounds_hbm, values_hbm, cells_hbm, far_ref, near_ref, own_ref, bounds, values, lines, wide, sems
):
    odd = lax.axis_index("zl")
    copies = [
        pltpu.make_async_copy(bounds_hbm, bounds, sems.at[0]),
        pltpu.make_async_copy(values_hbm, values, sems.at[1]),
        pltpu.make_async_copy(
            cells_hbm.at[pl.ds(pl.multiple_of(odd * COLS, COLS), CELL_ROWS)],
            far_ref.at[pl.ds(0, CELL_ROWS)],
            sems.at[2],
        ),
        pltpu.make_async_copy(
            cells_hbm.at[pl.ds(pl.multiple_of((1 - odd) * COLS, COLS), CELL_ROWS)],
            near_ref.at[pl.ds(0, CELL_ROWS)],
            sems.at[3],
        ),
    ]
    for copy in copies:
        copy.start()
    copies[0].wait()
    copies[1].wait()
    offset = lax.broadcasted_iota(jnp.int32, (NK, COLS), 1) - HALF
    for l in range(ROWS):
        for r in range(NR):
            inside = (offset >= bounds[l, 0, r]) & (offset <= bounds[l, 1, r])
            at = LINES * l + NK * r
            lines[at : at + NK, :] = jnp.where(inside, values[l, r], 0.0)
    lines[ROWS * LINES :, :] = jnp.zeros((192 - ROWS * LINES, COLS), jnp.float32)
    i = lax.broadcasted_iota(jnp.int32, (COLS, COLS), 0)
    j = lax.broadcasted_iota(jnp.int32, (COLS, COLS), 1)
    flip = ((i + j == 0) | (i + j == COLS)).astype(jnp.bfloat16)
    own_ref[...] = jnp.dot(
        lines[...].astype(jnp.bfloat16), flip, preferred_element_type=jnp.float32
    )
    wide[...] = jnp.zeros(wide.shape, jnp.float32)
    for place, above, below in packed_groups():
        for side, (row, r) in enumerate(((ROWS - RAD + above[0], above[1]), below)):
            at = LINES * row + NK * r
            wide[side, place : place + NK, :] = own_ref[at : at + NK, :]
    for side, ref in ((1 - odd, far_ref), (odd, near_ref)):
        for half in range(2):
            ref[CELL_ROWS:, half * COLS : (half + 1) * COLS] = wide[
                side, half * PACK_ROWS : (half + 1) * PACK_ROWS, :
            ].astype(jnp.bfloat16)
    copies[2].wait()
    copies[3].wait()


def own_kernel(cells_ref, lines_ref, field_ref, weight_ref, own_ref, lines_own, field_t, mixing):
    own_ref[...] = cells_ref[...]
    lines_own[...] = lines_ref[...]
    turned = field_ref[...].T
    field_t[:, : ROWS * COLS] = turned
    field_t[:, ROWS * COLS :] = turned
    for k in range(NK):
        mixing[k * CH : (k + 1) * CH, :] = weight_ref[k * CH : (k + 1) * CH, :].T


def rows_in_reach(up_ref, own_ref, down_ref):
    for n in range(RAD):
        yield up_ref[n * COLS : (n + 1) * COLS, :]
    for n in range(ROWS):
        yield own_ref[n]
    for n in range(RAD):
        yield down_ref[n * COLS : (n + 1) * COLS, :]


def by_parity(far_ref, near_ref, body):
    odd = lax.axis_index("zl")

    @pl.when(odd == 0)
    def _():
        body(far_ref, near_ref)

    @pl.when(odd == 1)
    def _():
        body(near_ref, far_ref)


def middle_kernel(far_ref, own_ref, near_ref, across_ref, beside_ref):
    first = pl.multiple_of(lax.axis_index("core") * HALF, HALF)
    other = pl.multiple_of(HALF - first, HALF)

    def halo(up_ref, down_ref):
        for n in range(RAD):
            across_ref[n] = up_ref[pl.ds(n * COLS + first, HALF), :]
            beside_ref[n] = up_ref[pl.ds(n * COLS + other, HALF), :]
            across_ref[RAD + ROWS + n] = down_ref[pl.ds(n * COLS + first, HALF), :]
            beside_ref[RAD + ROWS + n] = down_ref[pl.ds(n * COLS + other, HALF), :]

    by_parity(far_ref, near_ref, halo)
    for n in range(ROWS):
        across_ref[RAD + n] = own_ref[n, pl.ds(first, HALF), :]
        beside_ref[RAD + n] = own_ref[n, pl.ds(other, HALF), :]


def gather_lines(up_ref, own_ref, down_ref, lines_ref, wide):
    for side, ref in enumerate((up_ref, down_ref)):
        for half in range(2):
            wide[side, half * PACK_ROWS : (half + 1) * PACK_ROWS, :] = ref[
                CELL_ROWS:, half * COLS : (half + 1) * COLS
            ].astype(jnp.float32)
    for place, above, below in packed_groups():
        for side, (row, r) in enumerate((above, (RAD + ROWS + below[0], below[1]))):
            at = LINES * row + NK * r
            lines_ref[at : at + NK, :] = wide[side, place : place + NK, :]
    lines_ref[RAD * LINES : (RAD + ROWS) * LINES, :] = own_ref[: ROWS * LINES, :]


def own_mask():
    n = lax.broadcasted_iota(jnp.int32, (COLS, COLS), 0)
    i = lax.broadcasted_iota(jnp.int32, (COLS, COLS), 1)
    return ((i >= HALF) & (i > n)) | ((i < HALF) & (i <= n))


def fill_bands(inner_ref, outer_ref, lines_ref, inner_mask, outer_mask, l):
    for k in range(NK):
        for s in range(NR):
            at = LINES * (l + s) + NK * (NR - 1 - s) + k
            row = jnp.broadcast_to(lines_ref[pl.ds(at, 1), :], (16, COLS))
            base = pltpu.roll(row, 0, 1, stride=1, stride_axis=0).astype(jnp.bfloat16)
            for g in range(COLS // 16):
                tile = base if g == 0 else pltpu.roll(base, 16 * g, 1)
                rows = slice(k * COLS + 16 * g, k * COLS + 16 * (g + 1))
                cols = slice(s * COLS, (s + 1) * COLS)
                inner_ref[rows, cols] = tile * inner_mask[16 * g : 16 * (g + 1), :]
                outer_ref[rows, cols] = tile * outer_mask[16 * g : 16 * (g + 1), :]


def inner_kernel(
    far_ref, own_ref, near_ref, lines_own, part_ref, outer_ref, lines, wide, cells, bands
):
    def load(up_ref, down_ref):
        gather_lines(up_ref, lines_own, down_ref, lines, wide)
        for row, one in enumerate(rows_in_reach(up_ref, own_ref, down_ref)):
            cells[row * COLS : row * COLS + HALF, :] = one[HALF:]
            cells[row * COLS + HALF : (row + 1) * COLS, :] = one[:HALF]

    by_parity(far_ref, near_ref, load)
    mask = own_mask().astype(jnp.float32)
    inner_mask, outer_mask = mask.astype(jnp.bfloat16), (1.0 - mask).astype(jnp.bfloat16)
    for l in range(ROWS):
        band = bands.at[l % 2]
        fill_bands(band, outer_ref.at[l], lines, inner_mask, outer_mask, l)
        part_ref[l] = jnp.dot(
            band[...],
            cells[l * COLS : (l + NR) * COLS, :],
            preferred_element_type=jnp.float32,
        )


def outer_kernel(
    scale, bands, across, beside, part_ref, field_t, mixing, grad_hbm, gw_ref, cells, spreads, grad, sem
):
    first = pl.multiple_of(lax.axis_index("core") * HALF, HALF)
    other = pl.multiple_of(HALF - first, HALF)
    for row in range(EXT):
        cells[pl.ds(row * COLS + first, HALF), :] = across[row]
        cells[pl.ds(row * COLS + other, HALF), :] = beside[row]
    for l in range(ROWS):
        window = cells[l * COLS : (l + NR) * COLS, :]
        for k in range(NK):
            rows = slice(k * COLS, (k + 1) * COLS)
            spread = part_ref[l, rows, :] + jnp.dot(
                bands[l, rows, :], window, preferred_element_type=jnp.float32
            )
            high = spread.astype(jnp.bfloat16)
            low = (spread - high.astype(jnp.float32)).astype(jnp.bfloat16)
            at = slice(k * CH, (k + 1) * CH)
            spreads[l * COLS : (l + 1) * COLS, at] = high
            spreads[(ROWS + l) * COLS : (ROWS + l + 1) * COLS, at] = low
    grad[...] = jnp.dot(spreads[: ROWS * COLS, :], mixing[...], preferred_element_type=jnp.float32)
    store = pltpu.make_async_copy(grad, grad_hbm, sem)
    store.start()
    total = jnp.dot(field_t[...], spreads[...], preferred_element_type=jnp.float32) * scale
    for k in range(NK):
        gw_ref[k * CH : (k + 1) * CH, :] = total[:, k * CH : (k + 1) * CH].astype(jnp.bfloat16)
    store.wait()


def widen_kernel(sum_ref, out_hbm, wide, sems):
    copies = []
    for k in range(NK):
        rows = slice(k * CH, (k + 1) * CH)
        wide[rows, :] = sum_ref[rows, :].astype(jnp.float32)
        at = pl.ds(k * CH, CH)
        copies.append(pltpu.make_async_copy(wide.at[at], out_hbm.at[at], sems.at[k]))
        copies[-1].start()
    for copy in copies:
        copy.wait()


def exchange(x, axes):
    return lax.all_to_all(x, axes, 0, 0, tiled=True)


def per_device(field, cotangent, kernel_values, bounds, weight):
    sizes = {a: lax.axis_size(a) for a in LAT_AXES + LON_AXES}
    lat_count = math.prod(sizes[a] for a in LAT_AXES)
    lon_count = math.prod(sizes[a] for a in LON_AXES)
    params = pltpu.CompilerParams(vmem_limit_bytes=VMEM_LIMIT)
    hbm = pl.BlockSpec(memory_space=pltpu.HBM)
    wide = pltpu.VMEM((2, 2 * PACK_ROWS, COLS), jnp.float32)
    packed = jax.ShapeDtypeStruct((PACKED, CH), jnp.bfloat16)
    far, near, lines_own = pl.pallas_call(
        prep_kernel,
        out_shape=(packed, packed, jax.ShapeDtypeStruct((192, COLS), jnp.float32)),
        in_specs=[hbm, hbm, hbm],
        scratch_shapes=[
            pltpu.SMEM((ROWS, 2, NR), jnp.int32),
            pltpu.VMEM((ROWS, NR, NK, COLS), jnp.float32),
            pltpu.VMEM((192, COLS), jnp.float32),
            wide,
            pltpu.SemaphoreType.DMA((4,)),
        ],
        compiler_params=pltpu.CompilerParams(vmem_limit_bytes=60 * 1024 * 1024),
        name="prep",
    )(
        jnp.transpose(bounds, (1, 0, 2)),
        jnp.transpose(kernel_values, (1, 2, 0, 3)),
        cotangent.reshape(ROWS * COLS, CH),
    )
    own, lines_own, field_t, mixing = pl.pallas_call(
        own_kernel,
        out_shape=(
            jax.ShapeDtypeStruct(cotangent.shape, jnp.bfloat16),
            jax.ShapeDtypeStruct(lines_own.shape, jnp.float32),
            jax.ShapeDtypeStruct((CH, 2 * ROWS * COLS), jnp.bfloat16),
            jax.ShapeDtypeStruct((NK * CH, CH), jnp.bfloat16),
        ),
        compiler_params=params,
        cost_estimate=pl.CostEstimate(flops=0, bytes_accessed=4 * 1024 * 1024, transcendentals=0),
        name="own",
    )(cotangent, lines_own, field.reshape(ROWS * COLS, CH), weight)
    far = swapped(far, LAT_AXES, 1)
    near = swapped(near, LAT_AXES, 0)
    far, near, own, lines_own, field_t, mixing = lax.optimization_barrier(
        (far, near, own, lines_own, field_t, mixing)
    )
    side = jax.ShapeDtypeStruct((EXT, HALF, CH), jnp.bfloat16)
    across, beside = pl.pallas_call(
        middle_kernel, out_shape=(side, side), compiler_params=params, name="middle"
    )(far, own, near)
    across = lax.ppermute(
        across, LON_AXES, [(i, (i - 1 + 2 * (i % 2)) % lon_count) for i in range(lon_count)]
    )
    beside = lax.ppermute(beside, "core", [(0, 1), (1, 0)])

    cells = pltpu.VMEM((EXT * COLS, CH), jnp.bfloat16)
    band_flops = 2 * ROWS * NK * COLS * NR * COLS * CH
    part, bands = pl.pallas_call(
        inner_kernel,
        out_shape=(
            jax.ShapeDtypeStruct((ROWS, NK * COLS, CH), jnp.float32),
            jax.ShapeDtypeStruct((ROWS, NK * COLS, NR * COLS), jnp.bfloat16),
        ),
        scratch_shapes=[
            pltpu.VMEM((EXT * LINES, COLS), jnp.float32),
            wide,
            cells,
            pltpu.VMEM((2, NK * COLS, NR * COLS), jnp.bfloat16),
        ],
        compiler_params=params,
        cost_estimate=pl.CostEstimate(
            flops=band_flops, bytes_accessed=4 * 1024 * 1024, transcendentals=0
        ),
        name="inner_band",
    )(far, own, near, lines_own)

    scale = 1.0 / math.sqrt(ROWS * lat_count * COLS * lon_count)
    grad_field, gw = pl.pallas_call(
        functools.partial(outer_kernel, scale),
        out_shape=(
            jax.ShapeDtypeStruct((ROWS * COLS, CH), jnp.float32),
            jax.ShapeDtypeStruct((NK * CH, CH), jnp.bfloat16),
        ),
        out_specs=(hbm, pl.BlockSpec(memory_space=pltpu.VMEM)),
        scratch_shapes=[
            cells,
            pltpu.VMEM((2 * ROWS * COLS, NK * CH), jnp.bfloat16),
            pltpu.VMEM((ROWS * COLS, CH), jnp.float32),
            pltpu.SemaphoreType.DMA,
        ],
        compiler_params=params,
        cost_estimate=pl.CostEstimate(
            flops=band_flops * 2, bytes_accessed=6 * 1024 * 1024, transcendentals=0
        ),
        name="outer_band",
    )(bands, across, beside, part, field_t, mixing)

    near = math.prod(sizes[a] for a in NEAR)
    piece = gw.shape[0] // near
    got = exchange(gw.reshape(near, piece, CH), NEAR)
    for axes, count in ((DEPTH, math.prod(sizes[a] for a in DEPTH)), (NEAR, near)):
        mine = jnp.sum(got.astype(jnp.float32), axis=0).astype(jnp.bfloat16)
        got = exchange(jnp.broadcast_to(mine[None], (count, piece, CH)), axes)
    grad_weight = pl.pallas_call(
        widen_kernel,
        out_shape=jax.ShapeDtypeStruct((NK * CH, CH), jnp.float32),
        out_specs=hbm,
        scratch_shapes=[
            pltpu.VMEM((NK * CH, CH), jnp.float32),
            pltpu.SemaphoreType.DMA((NK,)),
        ],
        compiler_params=params,
        name="widen",
    )(got.reshape(NK * CH, CH))
    return (grad_field.reshape(ROWS, COLS, CH), grad_weight)


def solution(mesh):
    fine = Mesh(mesh.devices.reshape(2, 2, 2, 2, 2, 2, 4, 2), LAT_AXES + LON_AXES)
    return jax.shard_map(
        per_device,
        mesh=fine,
        in_specs=(
            P(LAT_AXES, LON_AXES, None),
            P(LAT_AXES, LON_AXES, None),
            P(None, LAT_AXES, None, None),
            P(None, LAT_AXES, None),
            P(),
        ),
        out_specs=(P(LAT_AXES, LON_AXES, None), P()),
        check_vma=False,
    )
```

```python
import functools
import math

import jax
import jax.numpy as jnp
from jax import lax
from jax.experimental import pallas as pl
from jax.experimental.pallas import tpu as pltpu
from jax.sharding import Mesh, PartitionSpec as P

LAT_AXES = ("yh", "z3", "z2", "z1", "zl")
LON_AXES = ("yl", "x", "core")
DEPTH = ("z1", "z2", "z3")
NEAR = ("yh", "zl", "yl", "x", "core")

ROWS, COLS, CH, NK, NR, RAD, HALF = 5, 128, 256, 4, 9, 4, 64
EXT = ROWS + 2 * RAD
LINES = NK * NR
CELL_ROWS = RAD * COLS
PACK_ROWS = 32
PACKED = CELL_ROWS + PACK_ROWS
VMEM_LIMIT = 32 * 1024 * 1024


def swapped(x, axes, start):
    count = math.prod(lax.axis_size(a) for a in axes)
    pairs = [(i, i + 1) for i in range(start, count - 1, 2)]
    return lax.ppermute(x, axes, pairs + [(j, i) for i, j in pairs])


def packed_groups():
    above = [(n, NR - 1 - n + t) for n in range(RAD) for t in range(n + 1)]
    below = [(n, t) for n in range(RAD) for t in range(RAD - n)]
    for place, (one, two) in enumerate(zip(above, below)):
        half = len(above) // 2
        yield (place // half) * PACK_ROWS + (place % half) * NK, one, two


def prep_kernel(
    bounds_hbm, values_hbm, cells_hbm, far_ref, near_ref, own_ref, bounds, values, lines, wide, sems
):
    odd = lax.axis_index("zl")
    copies = [
        pltpu.make_async_copy(bounds_hbm, bounds, sems.at[0]),
        pltpu.make_async_copy(values_hbm, values, sems.at[1]),
        pltpu.make_async_copy(
            cells_hbm.at[pl.ds(pl.multiple_of(odd * COLS, COLS), CELL_ROWS)],
            far_ref.at[pl.ds(0, CELL_ROWS)],
            sems.at[2],
        ),
        pltpu.make_async_copy(
            cells_hbm.at[pl.ds(pl.multiple_of((1 - odd) * COLS, COLS), CELL_ROWS)],
            near_ref.at[pl.ds(0, CELL_ROWS)],
            sems.at[3],
        ),
    ]
    for copy in copies:
        copy.start()
    copies[0].wait()
    copies[1].wait()
    offset = lax.broadcasted_iota(jnp.int32, (NK, COLS), 1) - HALF
    for l in range(ROWS):
        for r in range(NR):
            inside = (offset >= bounds[l, 0, r]) & (offset <= bounds[l, 1, r])
            at = LINES * l + NK * r
            lines[at : at + NK, :] = jnp.where(inside, values[l, r], 0.0)
    lines[ROWS * LINES :, :] = jnp.zeros((192 - ROWS * LINES, COLS), jnp.float32)
    i = lax.broadcasted_iota(jnp.int32, (COLS, COLS), 0)
    j = lax.broadcasted_iota(jnp.int32, (COLS, COLS), 1)
    flip = ((i + j == 0) | (i + j == COLS)).astype(jnp.bfloat16)
    own_ref[...] = jnp.dot(
        lines[...].astype(jnp.bfloat16), flip, preferred_element_type=jnp.float32
    )
    wide[...] = jnp.zeros(wide.shape, jnp.float32)
    for place, above, below in packed_groups():
        for side, (row, r) in enumerate(((ROWS - RAD + above[0], above[1]), below)):
            at = LINES * row + NK * r
            wide[side, place : place + NK, :] = own_ref[at : at + NK, :]
    for side, ref in ((1 - odd, far_ref), (odd, near_ref)):
        for half in range(2):
            ref[CELL_ROWS:, half * COLS : (half + 1) * COLS] = wide[
                side, half * PACK_ROWS : (half + 1) * PACK_ROWS, :
            ].astype(jnp.bfloat16)
    copies[2].wait()
    copies[3].wait()


def own_kernel(cells_ref, lines_ref, field_ref, weight_ref, own_ref, lines_own, field_t, mixing):
    own_ref[...] = cells_ref[...]
    lines_own[...] = lines_ref[...]
    turned = field_ref[...].T
    field_t[:, : ROWS * COLS] = turned
    field_t[:, ROWS * COLS :] = turned
    for k in range(NK):
        mixing[k * CH : (k + 1) * CH, :] = weight_ref[k * CH : (k + 1) * CH, :].T


def rows_in_reach(up_ref, own_ref, down_ref):
    for n in range(RAD):
        yield up_ref[n * COLS : (n + 1) * COLS, :]
    for n in range(ROWS):
        yield own_ref[n]
    for n in range(RAD):
        yield down_ref[n * COLS : (n + 1) * COLS, :]


def by_parity(far_ref, near_ref, body):
    odd = lax.axis_index("zl")

    @pl.when(odd == 0)
    def _():
        body(far_ref, near_ref)

    @pl.when(odd == 1)
    def _():
        body(near_ref, far_ref)


def middle_kernel(far_ref, own_ref, near_ref, across_ref, beside_ref):
    first = pl.multiple_of(lax.axis_index("core") * HALF, HALF)
    other = pl.multiple_of(HALF - first, HALF)

    def halo(up_ref, down_ref):
        for n in range(RAD):
            across_ref[n] = up_ref[pl.ds(n * COLS + first, HALF), :]
            beside_ref[n] = up_ref[pl.ds(n * COLS + other, HALF), :]
            across_ref[RAD + ROWS + n] = down_ref[pl.ds(n * COLS + first, HALF), :]
            beside_ref[RAD + ROWS + n] = down_ref[pl.ds(n * COLS + other, HALF), :]

    by_parity(far_ref, near_ref, halo)
    for n in range(ROWS):
        across_ref[RAD + n] = own_ref[n, pl.ds(first, HALF), :]
        beside_ref[RAD + n] = own_ref[n, pl.ds(other, HALF), :]


def gather_lines(up_ref, own_ref, down_ref, lines_ref, wide):
    for side, ref in enumerate((up_ref, down_ref)):
        for half in range(2):
            wide[side, half * PACK_ROWS : (half + 1) * PACK_ROWS, :] = ref[
                CELL_ROWS:, half * COLS : (half + 1) * COLS
            ].astype(jnp.float32)
    for place, above, below in packed_groups():
        for side, (row, r) in enumerate((above, (RAD + ROWS + below[0], below[1]))):
            at = LINES * row + NK * r
            lines_ref[at : at + NK, :] = wide[side, place : place + NK, :]
    lines_ref[RAD * LINES : (RAD + ROWS) * LINES, :] = own_ref[: ROWS * LINES, :]


def own_mask():
    n = lax.broadcasted_iota(jnp.int32, (COLS, COLS), 0)
    i = lax.broadcasted_iota(jnp.int32, (COLS, COLS), 1)
    return ((i >= HALF) & (i > n)) | ((i < HALF) & (i <= n))


def fill_bands(inner_ref, outer_ref, lines_ref, inner_mask, outer_mask, l):
    for k in range(NK):
        for s in range(NR):
            at = LINES * (l + s) + NK * (NR - 1 - s) + k
            row = jnp.broadcast_to(lines_ref[pl.ds(at, 1), :], (16, COLS))
            base = pltpu.roll(row, 0, 1, stride=1, stride_axis=0).astype(jnp.bfloat16)
            for g in range(COLS // 16):
                tile = base if g == 0 else pltpu.roll(base, 16 * g, 1)
                rows = slice(k * COLS + 16 * g, k * COLS + 16 * (g + 1))
                cols = slice(s * COLS, (s + 1) * COLS)
                inner_ref[rows, cols] = tile * inner_mask[16 * g : 16 * (g + 1), :]
                outer_ref[rows, cols] = tile * outer_mask[16 * g : 16 * (g + 1), :]


def inner_kernel(
    far_ref, own_ref, near_ref, lines_own, part_ref, outer_ref, lines, wide, cells, bands
):
    def load(up_ref, down_ref):
        gather_lines(up_ref, lines_own, down_ref, lines, wide)
        for row, one in enumerate(rows_in_reach(up_ref, own_ref, down_ref)):
            cells[row * COLS : row * COLS + HALF, :] = one[HALF:]
            cells[row * COLS + HALF : (row + 1) * COLS, :] = one[:HALF]

    by_parity(far_ref, near_ref, load)
    mask = own_mask().astype(jnp.float32)
    inner_mask, outer_mask = mask.astype(jnp.bfloat16), (1.0 - mask).astype(jnp.bfloat16)
    for l in range(ROWS):
        band = bands.at[l % 2]
        fill_bands(band, outer_ref.at[l], lines, inner_mask, outer_mask, l)
        window = cells[l * COLS : (l + NR) * COLS, :]
        for k in range(NK):
            rows = slice(k * COLS, (k + 1) * COLS)
            part_ref[l, rows, :] = jnp.dot(
                band[rows, :], window, preferred_element_type=jnp.float32
            )


def outer_kernel(
    scale, bands, across, beside, part_ref, field_t, mixing, grad_hbm, gw_ref, cells, spreads, grad, sem
):
    first = pl.multiple_of(lax.axis_index("core") * HALF, HALF)
    other = pl.multiple_of(HALF - first, HALF)
    for row in range(EXT):
        cells[pl.ds(row * COLS + first, HALF), :] = across[row]
        cells[pl.ds(row * COLS + other, HALF), :] = beside[row]
    for l in range(ROWS):
        window = cells[l * COLS : (l + NR) * COLS, :]
        for k in range(NK):
            rows = slice(k * COLS, (k + 1) * COLS)
            spread = part_ref[l, rows, :] + jnp.dot(
                bands[l, rows, :], window, preferred_element_type=jnp.float32
            )
            high = spread.astype(jnp.bfloat16)
            low = (spread - high.astype(jnp.float32)).astype(jnp.bfloat16)
            at = slice(k * CH, (k + 1) * CH)
            spreads[l * COLS : (l + 1) * COLS, at] = high
            spreads[(ROWS + l) * COLS : (ROWS + l + 1) * COLS, at] = low
    grad[...] = jnp.dot(spreads[: ROWS * COLS, :], mixing[...], preferred_element_type=jnp.float32)
    store = pltpu.make_async_copy(grad, grad_hbm, sem)
    store.start()
    total = jnp.dot(field_t[...], spreads[...], preferred_element_type=jnp.float32) * scale
    for k in range(NK):
        gw_ref[k * CH : (k + 1) * CH, :] = total[:, k * CH : (k + 1) * CH].astype(jnp.bfloat16)
    store.wait()


def widen_kernel(sum_ref, out_hbm, wide, sems):
    copies = []
    for k in range(NK):
        rows = slice(k * CH, (k + 1) * CH)
        wide[rows, :] = sum_ref[rows, :].astype(jnp.float32)
        at = pl.ds(k * CH, CH)
        copies.append(pltpu.make_async_copy(wide.at[at], out_hbm.at[at], sems.at[k]))
        copies[-1].start()
    for copy in copies:
        copy.wait()


def exchange(x, axes):
    return lax.all_to_all(x, axes, 0, 0, tiled=True)


def per_device(field, cotangent, kernel_values, bounds, weight):
    sizes = {a: lax.axis_size(a) for a in LAT_AXES + LON_AXES}
    lat_count = math.prod(sizes[a] for a in LAT_AXES)
    lon_count = math.prod(sizes[a] for a in LON_AXES)
    params = pltpu.CompilerParams(vmem_limit_bytes=VMEM_LIMIT)
    hbm = pl.BlockSpec(memory_space=pltpu.HBM)
    wide = pltpu.VMEM((2, 2 * PACK_ROWS, COLS), jnp.float32)
    packed = jax.ShapeDtypeStruct((PACKED, CH), jnp.bfloat16)
    far, near, lines_own = pl.pallas_call(
        prep_kernel,
        out_shape=(packed, packed, jax.ShapeDtypeStruct((192, COLS), jnp.float32)),
        in_specs=[hbm, hbm, hbm],
        scratch_shapes=[
            pltpu.SMEM((ROWS, 2, NR), jnp.int32),
            pltpu.VMEM((ROWS, NR, NK, COLS), jnp.float32),
            pltpu.VMEM((192, COLS), jnp.float32),
            wide,
            pltpu.SemaphoreType.DMA((4,)),
        ],
        compiler_params=pltpu.CompilerParams(vmem_limit_bytes=60 * 1024 * 1024),
        name="prep",
    )(
        jnp.transpose(bounds, (1, 0, 2)),
        jnp.transpose(kernel_values, (1, 2, 0, 3)),
        cotangent.reshape(ROWS * COLS, CH),
    )
    own, lines_own, field_t, mixing = pl.pallas_call(
        own_kernel,
        out_shape=(
            jax.ShapeDtypeStruct(cotangent.shape, jnp.bfloat16),
            jax.ShapeDtypeStruct(lines_own.shape, jnp.float32),
            jax.ShapeDtypeStruct((CH, 2 * ROWS * COLS), jnp.bfloat16),
            jax.ShapeDtypeStruct((NK * CH, CH), jnp.bfloat16),
        ),
        compiler_params=params,
        cost_estimate=pl.CostEstimate(flops=0, bytes_accessed=4 * 1024 * 1024, transcendentals=0),
        name="own",
    )(cotangent, lines_own, field.reshape(ROWS * COLS, CH), weight)
    far = swapped(far, LAT_AXES, 1)
    near = swapped(near, LAT_AXES, 0)
    far, near, own, lines_own, field_t, mixing = lax.optimization_barrier(
        (far, near, own, lines_own, field_t, mixing)
    )
    side = jax.ShapeDtypeStruct((EXT, HALF, CH), jnp.bfloat16)
    across, beside = pl.pallas_call(
        middle_kernel, out_shape=(side, side), compiler_params=params, name="middle"
    )(far, own, near)
    across = lax.ppermute(
        across, LON_AXES, [(i, (i - 1 + 2 * (i % 2)) % lon_count) for i in range(lon_count)]
    )
    beside = lax.ppermute(beside, "core", [(0, 1), (1, 0)])

    cells = pltpu.VMEM((EXT * COLS, CH), jnp.bfloat16)
    band_flops = 2 * ROWS * NK * COLS * NR * COLS * CH
    part, bands = pl.pallas_call(
        inner_kernel,
        out_shape=(
            jax.ShapeDtypeStruct((ROWS, NK * COLS, CH), jnp.float32),
            jax.ShapeDtypeStruct((ROWS, NK * COLS, NR * COLS), jnp.bfloat16),
        ),
        scratch_shapes=[
            pltpu.VMEM((EXT * LINES, COLS), jnp.float32),
            wide,
            cells,
            pltpu.VMEM((2, NK * COLS, NR * COLS), jnp.bfloat16),
        ],
        compiler_params=params,
        cost_estimate=pl.CostEstimate(
            flops=band_flops, bytes_accessed=4 * 1024 * 1024, transcendentals=0
        ),
        name="inner_band",
    )(far, own, near, lines_own)

    scale = 1.0 / math.sqrt(ROWS * lat_count * COLS * lon_count)
    grad_field, gw = pl.pallas_call(
        functools.partial(outer_kernel, scale),
        out_shape=(
            jax.ShapeDtypeStruct((ROWS * COLS, CH), jnp.float32),
            jax.ShapeDtypeStruct((NK * CH, CH), jnp.bfloat16),
        ),
        out_specs=(hbm, pl.BlockSpec(memory_space=pltpu.VMEM)),
        scratch_shapes=[
            cells,
            pltpu.VMEM((2 * ROWS * COLS, NK * CH), jnp.bfloat16),
            pltpu.VMEM((ROWS * COLS, CH), jnp.float32),
            pltpu.SemaphoreType.DMA,
        ],
        compiler_params=params,
        cost_estimate=pl.CostEstimate(
            flops=band_flops * 2, bytes_accessed=6 * 1024 * 1024, transcendentals=0
        ),
        name="outer_band",
    )(bands, across, beside, part, field_t, mixing)

    near = math.prod(sizes[a] for a in NEAR)
    piece = gw.shape[0] // near
    got = exchange(gw.reshape(near, piece, CH), NEAR)
    for axes, count in ((DEPTH, math.prod(sizes[a] for a in DEPTH)), (NEAR, near)):
        mine = jnp.sum(got.astype(jnp.float32), axis=0).astype(jnp.bfloat16)
        got = exchange(jnp.broadcast_to(mine[None], (count, piece, CH)), axes)
    grad_weight = pl.pallas_call(
        widen_kernel,
        out_shape=jax.ShapeDtypeStruct((NK * CH, CH), jnp.float32),
        out_specs=hbm,
        scratch_shapes=[
            pltpu.VMEM((NK * CH, CH), jnp.float32),
            pltpu.SemaphoreType.DMA((NK,)),
        ],
        compiler_params=params,
        name="widen",
    )(got.reshape(NK * CH, CH))
    return (grad_field.reshape(ROWS, COLS, CH), grad_weight)


def solution(mesh):
    fine = Mesh(mesh.devices.reshape(2, 2, 2, 2, 2, 2, 4, 2), LAT_AXES + LON_AXES)
    return jax.shard_map(
        per_device,
        mesh=fine,
        in_specs=(
            P(LAT_AXES, LON_AXES, None),
            P(LAT_AXES, LON_AXES, None),
            P(None, LAT_AXES, None, None),
            P(None, LAT_AXES, None),
            P(),
        ),
        out_specs=(P(LAT_AXES, LON_AXES, None), P()),
        check_vma=False,
    )
```

```python
import functools
import math

import jax
import jax.numpy as jnp
from jax import lax
from jax.experimental import pallas as pl
from jax.experimental.pallas import tpu as pltpu
from jax.sharding import Mesh, PartitionSpec as P

LAT_AXES = ("yh", "z3", "z2", "z1", "zl")
LON_AXES = ("yl", "x", "core")
DEPTH = ("z1", "z2", "z3")
NEAR = ("yh", "zl", "yl", "x", "core")

ROWS, COLS, CH, NK, NR, RAD, HALF = 5, 128, 256, 4, 9, 4, 64
EXT = ROWS + 2 * RAD
LINES = NK * NR
CELL_ROWS = RAD * COLS
PACK_ROWS = 32
PACKED = CELL_ROWS + PACK_ROWS
VMEM_LIMIT = 32 * 1024 * 1024


def swapped(x, axes, start):
    count = math.prod(lax.axis_size(a) for a in axes)
    pairs = [(i, i + 1) for i in range(start, count - 1, 2)]
    return lax.ppermute(x, axes, pairs + [(j, i) for i, j in pairs])


def packed_groups():
    above = [(n, NR - 1 - n + t) for n in range(RAD) for t in range(n + 1)]
    below = [(n, t) for n in range(RAD) for t in range(RAD - n)]
    for place, (one, two) in enumerate(zip(above, below)):
        half = len(above) // 2
        yield (place // half) * PACK_ROWS + (place % half) * NK, one, two


def prep_kernel(
    bounds_hbm, values_hbm, cells_hbm, far_ref, near_ref, own_ref, bounds, values, lines, wide, sems
):
    odd = lax.axis_index("zl")
    copies = [
        pltpu.make_async_copy(bounds_hbm, bounds, sems.at[0]),
        pltpu.make_async_copy(values_hbm, values, sems.at[1]),
        pltpu.make_async_copy(
            cells_hbm.at[pl.ds(pl.multiple_of(odd * COLS, COLS), CELL_ROWS)],
            far_ref.at[pl.ds(0, CELL_ROWS)],
            sems.at[2],
        ),
        pltpu.make_async_copy(
            cells_hbm.at[pl.ds(pl.multiple_of((1 - odd) * COLS, COLS), CELL_ROWS)],
            near_ref.at[pl.ds(0, CELL_ROWS)],
            sems.at[3],
        ),
    ]
    for copy in copies:
        copy.start()
    copies[0].wait()
    copies[1].wait()
    offset = lax.broadcasted_iota(jnp.int32, (NK, COLS), 1) - HALF
    for l in range(ROWS):
        for r in range(NR):
            inside = (offset >= bounds[l, 0, r]) & (offset <= bounds[l, 1, r])
            at = LINES * l + NK * r
            lines[at : at + NK, :] = jnp.where(inside, values[l, r], 0.0)
    lines[ROWS * LINES :, :] = jnp.zeros((192 - ROWS * LINES, COLS), jnp.float32)
    i = lax.broadcasted_iota(jnp.int32, (COLS, COLS), 0)
    j = lax.broadcasted_iota(jnp.int32, (COLS, COLS), 1)
    flip = ((i + j == 0) | (i + j == COLS)).astype(jnp.bfloat16)
    own_ref[...] = jnp.dot(
        lines[...].astype(jnp.bfloat16), flip, preferred_element_type=jnp.float32
    )
    wide[...] = jnp.zeros(wide.shape, jnp.float32)
    for place, above, below in packed_groups():
        for side, (row, r) in enumerate(((ROWS - RAD + above[0], above[1]), below)):
            at = LINES * row + NK * r
            wide[side, place : place + NK, :] = own_ref[at : at + NK, :]
    for side, ref in ((1 - odd, far_ref), (odd, near_ref)):
        for half in range(2):
            ref[CELL_ROWS:, half * COLS : (half + 1) * COLS] = wide[
                side, half * PACK_ROWS : (half + 1) * PACK_ROWS, :
            ].astype(jnp.bfloat16)
    copies[2].wait()
    copies[3].wait()


def own_kernel(cells_ref, lines_ref, field_ref, weight_ref, own_ref, lines_own, field_t, mixing):
    own_ref[...] = cells_ref[...]
    lines_own[...] = lines_ref[...]
    turned = field_ref[...].T
    field_t[:, : ROWS * COLS] = turned
    field_t[:, ROWS * COLS :] = turned
    for k in range(NK):
        mixing[k * CH : (k + 1) * CH, :] = weight_ref[k * CH : (k + 1) * CH, :].T


def rows_in_reach(up_ref, own_ref, down_ref):
    for n in range(RAD):
        yield up_ref[n * COLS : (n + 1) * COLS, :]
    for n in range(ROWS):
        yield own_ref[n]
    for n in range(RAD):
        yield down_ref[n * COLS : (n + 1) * COLS, :]


def by_parity(far_ref, near_ref, body):
    odd = lax.axis_index("zl")

    @pl.when(odd == 0)
    def _():
        body(far_ref, near_ref)

    @pl.when(odd == 1)
    def _():
        body(near_ref, far_ref)


def middle_kernel(far_ref, own_ref, near_ref, across_ref, beside_ref):
    first = pl.multiple_of(lax.axis_index("core") * HALF, HALF)
    other = pl.multiple_of(HALF - first, HALF)

    def halo(up_ref, down_ref):
        for n in range(RAD):
            across_ref[n] = up_ref[pl.ds(n * COLS + first, HALF), :]
            beside_ref[n] = up_ref[pl.ds(n * COLS + other, HALF), :]
            across_ref[RAD + ROWS + n] = down_ref[pl.ds(n * COLS + first, HALF), :]
            beside_ref[RAD + ROWS + n] = down_ref[pl.ds(n * COLS + other, HALF), :]

    by_parity(far_ref, near_ref, halo)
    for n in range(ROWS):
        across_ref[RAD + n] = own_ref[n, pl.ds(first, HALF), :]
        beside_ref[RAD + n] = own_ref[n, pl.ds(other, HALF), :]


def gather_lines(up_ref, own_ref, down_ref, lines_ref, wide):
    for side, ref in enumerate((up_ref, down_ref)):
        for half in range(2):
            wide[side, half * PACK_ROWS : (half + 1) * PACK_ROWS, :] = ref[
                CELL_ROWS:, half * COLS : (half + 1) * COLS
            ].astype(jnp.float32)
    for place, above, below in packed_groups():
        for side, (row, r) in enumerate((above, (RAD + ROWS + below[0], below[1]))):
            at = LINES * row + NK * r
            lines_ref[at : at + NK, :] = wide[side, place : place + NK, :]
    lines_ref[RAD * LINES : (RAD + ROWS) * LINES, :] = own_ref[: ROWS * LINES, :]


def own_mask():
    n = lax.broadcasted_iota(jnp.int32, (COLS, COLS), 0)
    i = lax.broadcasted_iota(jnp.int32, (COLS, COLS), 1)
    return ((i >= HALF) & (i > n)) | ((i < HALF) & (i <= n))


def fill_bands(inner_ref, outer_ref, lines_ref, inner_mask, outer_mask, l):
    for k in range(NK):
        for s in range(NR):
            at = LINES * (l + s) + NK * (NR - 1 - s) + k
            row = jnp.broadcast_to(lines_ref[pl.ds(at, 1), :], (16, COLS))
            base = pltpu.roll(row, 0, 1, stride=1, stride_axis=0).astype(jnp.bfloat16)
            for g in range(COLS // 16):
                tile = base if g == 0 else pltpu.roll(base, 16 * g, 1)
                rows = slice(k * COLS + 16 * g, k * COLS + 16 * (g + 1))
                cols = slice(s * COLS, (s + 1) * COLS)
                inner_ref[rows, cols] = tile * inner_mask[16 * g : 16 * (g + 1), :]
                outer_ref[rows, cols] = tile * outer_mask[16 * g : 16 * (g + 1), :]


def inner_kernel(
    far_ref, own_ref, near_ref, lines_own, part_ref, outer_ref, lines, wide, cells, bands
):
    def load(up_ref, down_ref):
        gather_lines(up_ref, lines_own, down_ref, lines, wide)
        for row, one in enumerate(rows_in_reach(up_ref, own_ref, down_ref)):
            cells[row * COLS : row * COLS + HALF, :] = one[HALF:]
            cells[row * COLS + HALF : (row + 1) * COLS, :] = one[:HALF]

    by_parity(far_ref, near_ref, load)
    mask = own_mask().astype(jnp.float32)
    inner_mask, outer_mask = mask.astype(jnp.bfloat16), (1.0 - mask).astype(jnp.bfloat16)
    for l in range(ROWS):
        band = bands.at[l]
        fill_bands(band, outer_ref.at[l], lines, inner_mask, outer_mask, l)
        part_ref[l] = jnp.dot(
            band[...],
            cells[l * COLS : (l + NR) * COLS, :],
            preferred_element_type=jnp.float32,
        )


def outer_kernel(
    scale, bands, across, beside, part_ref, field_t, mixing, grad_hbm, gw_ref, cells, spreads, grad, sem
):
    first = pl.multiple_of(lax.axis_index("core") * HALF, HALF)
    other = pl.multiple_of(HALF - first, HALF)
    for row in range(EXT):
        cells[pl.ds(row * COLS + first, HALF), :] = across[row]
        cells[pl.ds(row * COLS + other, HALF), :] = beside[row]
    for l in range(ROWS):
        window = cells[l * COLS : (l + NR) * COLS, :]
        for k in range(NK):
            rows = slice(k * COLS, (k + 1) * COLS)
            spread = part_ref[l, rows, :] + jnp.dot(
                bands[l, rows, :], window, preferred_element_type=jnp.float32
            )
            high = spread.astype(jnp.bfloat16)
            low = (spread - high.astype(jnp.float32)).astype(jnp.bfloat16)
            at = slice(k * CH, (k + 1) * CH)
            spreads[l * COLS : (l + 1) * COLS, at] = high
            spreads[(ROWS + l) * COLS : (ROWS + l + 1) * COLS, at] = low
    grad[...] = jnp.dot(spreads[: ROWS * COLS, :], mixing[...], preferred_element_type=jnp.float32)
    store = pltpu.make_async_copy(grad, grad_hbm, sem)
    store.start()
    total = jnp.dot(field_t[...], spreads[...], preferred_element_type=jnp.float32) * scale
    for k in range(NK):
        gw_ref[k * CH : (k + 1) * CH, :] = total[:, k * CH : (k + 1) * CH].astype(jnp.bfloat16)
    store.wait()


def widen_kernel(sum_ref, out_hbm, wide, sems):
    copies = []
    for k in range(NK):
        rows = slice(k * CH, (k + 1) * CH)
        wide[rows, :] = sum_ref[rows, :].astype(jnp.float32)
        at = pl.ds(k * CH, CH)
        copies.append(pltpu.make_async_copy(wide.at[at], out_hbm.at[at], sems.at[k]))
        copies[-1].start()
    for copy in copies:
        copy.wait()


def exchange(x, axes):
    return lax.all_to_all(x, axes, 0, 0, tiled=True)


def per_device(field, cotangent, kernel_values, bounds, weight):
    sizes = {a: lax.axis_size(a) for a in LAT_AXES + LON_AXES}
    lat_count = math.prod(sizes[a] for a in LAT_AXES)
    lon_count = math.prod(sizes[a] for a in LON_AXES)
    params = pltpu.CompilerParams(vmem_limit_bytes=VMEM_LIMIT)
    hbm = pl.BlockSpec(memory_space=pltpu.HBM)
    wide = pltpu.VMEM((2, 2 * PACK_ROWS, COLS), jnp.float32)
    packed = jax.ShapeDtypeStruct((PACKED, CH), jnp.bfloat16)
    far, near, lines_own = pl.pallas_call(
        prep_kernel,
        out_shape=(packed, packed, jax.ShapeDtypeStruct((192, COLS), jnp.float32)),
        in_specs=[hbm, hbm, hbm],
        scratch_shapes=[
            pltpu.SMEM((ROWS, 2, NR), jnp.int32),
            pltpu.VMEM((ROWS, NR, NK, COLS), jnp.float32),
            pltpu.VMEM((192, COLS), jnp.float32),
            wide,
            pltpu.SemaphoreType.DMA((4,)),
        ],
        compiler_params=pltpu.CompilerParams(vmem_limit_bytes=60 * 1024 * 1024),
        name="prep",
    )(
        jnp.transpose(bounds, (1, 0, 2)),
        jnp.transpose(kernel_values, (1, 2, 0, 3)),
        cotangent.reshape(ROWS * COLS, CH),
    )
    own, lines_own, field_t, mixing = pl.pallas_call(
        own_kernel,
        out_shape=(
            jax.ShapeDtypeStruct(cotangent.shape, jnp.bfloat16),
            jax.ShapeDtypeStruct(lines_own.shape, jnp.float32),
            jax.ShapeDtypeStruct((CH, 2 * ROWS * COLS), jnp.bfloat16),
            jax.ShapeDtypeStruct((NK * CH, CH), jnp.bfloat16),
        ),
        compiler_params=params,
        cost_estimate=pl.CostEstimate(flops=0, bytes_accessed=4 * 1024 * 1024, transcendentals=0),
        name="own",
    )(cotangent, lines_own, field.reshape(ROWS * COLS, CH), weight)
    far = swapped(far, LAT_AXES, 1)
    near = swapped(near, LAT_AXES, 0)
    far, near, own, lines_own, field_t, mixing = lax.optimization_barrier(
        (far, near, own, lines_own, field_t, mixing)
    )
    side = jax.ShapeDtypeStruct((EXT, HALF, CH), jnp.bfloat16)
    across, beside = pl.pallas_call(
        middle_kernel, out_shape=(side, side), compiler_params=params, name="middle"
    )(far, own, near)
    across = lax.ppermute(
        across, LON_AXES, [(i, (i - 1 + 2 * (i % 2)) % lon_count) for i in range(lon_count)]
    )
    beside = lax.ppermute(beside, "core", [(0, 1), (1, 0)])

    cells = pltpu.VMEM((EXT * COLS, CH), jnp.bfloat16)
    band_flops = 2 * ROWS * NK * COLS * NR * COLS * CH
    part, bands = pl.pallas_call(
        inner_kernel,
        out_shape=(
            jax.ShapeDtypeStruct((ROWS, NK * COLS, CH), jnp.float32),
            jax.ShapeDtypeStruct((ROWS, NK * COLS, NR * COLS), jnp.bfloat16),
        ),
        scratch_shapes=[
            pltpu.VMEM((EXT * LINES, COLS), jnp.float32),
            wide,
            cells,
            pltpu.VMEM((ROWS, NK * COLS, NR * COLS), jnp.bfloat16),
        ],
        compiler_params=params,
        cost_estimate=pl.CostEstimate(
            flops=band_flops, bytes_accessed=4 * 1024 * 1024, transcendentals=0
        ),
        name="inner_band",
    )(far, own, near, lines_own)

    scale = 1.0 / math.sqrt(ROWS * lat_count * COLS * lon_count)
    grad_field, gw = pl.pallas_call(
        functools.partial(outer_kernel, scale),
        out_shape=(
            jax.ShapeDtypeStruct((ROWS * COLS, CH), jnp.float32),
            jax.ShapeDtypeStruct((NK * CH, CH), jnp.bfloat16),
        ),
        out_specs=(hbm, pl.BlockSpec(memory_space=pltpu.VMEM)),
        scratch_shapes=[
            cells,
            pltpu.VMEM((2 * ROWS * COLS, NK * CH), jnp.bfloat16),
            pltpu.VMEM((ROWS * COLS, CH), jnp.float32),
            pltpu.SemaphoreType.DMA,
        ],
        compiler_params=params,
        cost_estimate=pl.CostEstimate(
            flops=band_flops * 2, bytes_accessed=6 * 1024 * 1024, transcendentals=0
        ),
        name="outer_band",
    )(bands, across, beside, part, field_t, mixing)

    near = math.prod(sizes[a] for a in NEAR)
    piece = gw.shape[0] // near
    got = exchange(gw.reshape(near, piece, CH), NEAR)
    for axes, count in ((DEPTH, math.prod(sizes[a] for a in DEPTH)), (NEAR, near)):
        mine = jnp.sum(got.astype(jnp.float32), axis=0).astype(jnp.bfloat16)
        got = exchange(jnp.broadcast_to(mine[None], (count, piece, CH)), axes)
    grad_weight = pl.pallas_call(
        widen_kernel,
        out_shape=jax.ShapeDtypeStruct((NK * CH, CH), jnp.float32),
        out_specs=hbm,
        scratch_shapes=[
            pltpu.VMEM((NK * CH, CH), jnp.float32),
            pltpu.SemaphoreType.DMA((NK,)),
        ],
        compiler_params=params,
        name="widen",
    )(got.reshape(NK * CH, CH))
    return (grad_field.reshape(ROWS, COLS, CH), grad_weight)


def solution(mesh):
    fine = Mesh(mesh.devices.reshape(2, 2, 2, 2, 2, 2, 4, 2), LAT_AXES + LON_AXES)
    return jax.shard_map(
        per_device,
        mesh=fine,
        in_specs=(
            P(LAT_AXES, LON_AXES, None),
            P(LAT_AXES, LON_AXES, None),
            P(None, LAT_AXES, None, None),
            P(None, LAT_AXES, None),
            P(),
        ),
        out_specs=(P(LAT_AXES, LON_AXES, None), P()),
        check_vma=False,
    )
```
